32 devices in a mesh: ctx: 8 (over y, x, core), wt: 4 (over z).
Axes of the slice: x: 2, y: 2, z: 4, core: 2. Of those that a mesh axis runs over, the one named last changes fastest.
Arguments:
- inputs: bfloat16 [4, 3584, 768], P('wt', 'ctx'), may hold values from -6 to 6
- block_table: int32 [8, 2], replicated, may hold values from 0 to 15, as said below
- ln1_gain: bfloat16 [2, 768], P(None, 'wt'), may hold values from 0.5 to 1.5
- ln1_bias: bfloat16 [2, 768], P(None, 'wt'), may hold values from -1 to 1
- qkv_weight: bfloat16 [2, 768, 2304], P(None, 'wt'), may hold values from -0.21875 to 0.21875
- query_bias: bfloat16 [2, 768], P(None, 'wt'), may hold values from -1 to 1
- value_bias: bfloat16 [2, 768], P(None, 'wt'), may hold values from -0.25 to 0.25
- out_weight: bfloat16 [2, 768, 768], P(None, 'wt'), may hold values from -0.875 to 0.875
- out_bias: bfloat16 [2, 768], P(None, 'wt'), may hold values from -1 to 1
- ln2_gain: bfloat16 [2, 768], P(None, 'wt'), may hold values from 0.5 to 1.5
- ln2_bias: bfloat16 [2, 768], P(None, 'wt'), may hold values from -1 to 1
- up_weight: bfloat16 [2, 768, 3072], P(None, 'wt'), may hold values from -0.21875 to 0.21875
- up_bias: bfloat16 [2, 3072], P(None, 'wt'), may hold values from -1 to 1
- down_weight: bfloat16 [2, 3072, 768], P(None, 'wt'), may hold values from -0.109375 to 0.109375
- down_bias: bfloat16 [2, 768], P(None, 'wt'), may hold values from -1 to 1
- cotangent: bfloat16 [4, 3584, 768], P('wt', 'ctx'), may hold values from -6 to 6
Outputs:
- outputs: bfloat16 [4, 3584, 768], P('wt', 'ctx')
- inputs_grad: float32 [4, 3584, 768], P('wt', 'ctx')
- ln1_gain_grad: float32 [2, 768], P(None, 'wt')
- ln1_bias_grad: float32 [2, 768], P(None, 'wt')
- qkv_weight_grad: float32 [2, 768, 2304], P(None, 'wt')
- query_bias_grad: float32 [2, 768], P(None, 'wt')
- value_bias_grad: float32 [2, 768], P(None, 'wt')
- out_weight_grad: float32 [2, 768, 768], P(None, 'wt')
- out_bias_grad: float32 [2, 768], P(None, 'wt')
- ln2_gain_grad: float32 [2, 768], P(None, 'wt')
- ln2_bias_grad: float32 [2, 768], P(None, 'wt')
- up_weight_grad: float32 [2, 768, 3072], P(None, 'wt')
- up_bias_grad: float32 [2, 3072], P(None, 'wt')
- down_weight_grad: float32 [2, 3072, 768], P(None, 'wt')
- down_bias_grad: float32 [2, 768], P(None, 'wt')
The draws below stay inside these ranges and needn't reach their ends.
Inputs may be any that keep to these rules, and one draw needn't show every extreme that they name: `block_table`: row c holds p and 15 - p for some p < 8; the first column is a permutation of 0 to 7.
All inputs are finite; a program needn't handle non-finite values.
Results may differ from the reference program's by a relative error of at most 0.011.
Values may be sent and summed in bfloat16 or wider, within the bound.
No kernel may reach another device: no remote copies, remote signals or barrier semaphores. Data moves between devices by JAX's collectives and lax.ppermute only.
A program may use at most 320 MiB of HBM per device.

```python
import jax
import jax.numpy as jnp
from jax import lax

D = 768
HEAD_DIM = 64
FF = 3072
LAYERS = 2
BLK = 224
LEN = 3584
NSEQ = 4
N_CTX = 8


def draw_block_table(key, part):
    first = jax.random.permutation(key, N_CTX).astype(jnp.int32)
    return jnp.stack([first, 2 * N_CTX - 1 - first], axis=1)


def steps_of(own_key, shape, split, least, high):
    level = 1.0
    for axis_at, blocks in split:
        draws = jax.random.uniform(jax.random.fold_in(jax.random.fold_in(own_key, 6), axis_at), (blocks,), jnp.float32, least / len(split), high / len(split))
        level = level * jnp.repeat(jnp.exp(draws), shape[axis_at] // blocks).reshape((-1,) + (1,) * (len(shape) - 1 - axis_at))
    return level


def bell_draw(key, shape, spread, reach, pieces=(), kind=jnp.bfloat16):
    values = jax.random.normal(key, shape, jnp.float32) * spread
    if len(pieces) > 0:
        values = steps_of(key, shape, pieces, -0.22, 0.18) * values
    return jnp.clip(values, min=-reach, max=reach).astype(kind)


def setup_inputs(seed: int = 0) -> dict:
    arg_keys = jax.random.split(jax.random.key(seed), 17)
    inputs = bell_draw(arg_keys[0], (NSEQ, LEN, D), 1.0, 6.0, ((0, 4), (1, 8)))
    block_table = draw_block_table(jax.random.fold_in(arg_keys[16], 71), 0)
    ln1_gain = jnp.clip(1.0 + 0.1 * jax.random.normal(arg_keys[2], (LAYERS, D), jnp.float32), 0.5, 1.5).astype(jnp.bfloat16)
    ln1_bias = bell_draw(arg_keys[3], (LAYERS, D), 0.2, 1.0, ((1, 4),))
    qkv_weight = bell_draw(arg_keys[4], (LAYERS, D, 3 * D), D ** -0.5, 0.21875, ((1, 4),))
    query_bias = bell_draw(arg_keys[5], (LAYERS, D), 0.2, 1.0, ((1, 4),))
    value_bias = bell_draw(arg_keys[6], (LAYERS, D), 0.05, 0.25, ((1, 4),))
    out_weight = bell_draw(arg_keys[7], (LAYERS, D, D), (D // 16) ** -0.5, 0.875, ((1, 4),))
    out_bias = bell_draw(arg_keys[8], (LAYERS, D), 0.2, 1.0, ((1, 4),))
    ln2_gain = jnp.clip(1.0 + 0.1 * jax.random.normal(arg_keys[9], (LAYERS, D), jnp.float32), 0.5, 1.5).astype(jnp.bfloat16)
    ln2_bias = bell_draw(arg_keys[10], (LAYERS, D), 0.2, 1.0, ((1, 4),))
    up_weight = bell_draw(arg_keys[11], (LAYERS, D, FF), D ** -0.5, 0.21875, ((1, 4),))
    up_bias = bell_draw(arg_keys[12], (LAYERS, FF), 0.2, 1.0, ((1, 4),))
    down_weight = bell_draw(arg_keys[13], (LAYERS, FF, D), FF ** -0.5, 0.109375, ((1, 4),))
    down_bias = bell_draw(arg_keys[14], (LAYERS, D), 0.2, 1.0, ((1, 4),))
    cotangent = bell_draw(arg_keys[15], (NSEQ, LEN, D), 1.0, 6.0, ((0, 4), (1, 8)))
    return {"inputs": inputs, "block_table": block_table, "ln1_gain": ln1_gain, "ln1_bias": ln1_bias, "qkv_weight": qkv_weight, "query_bias": query_bias, "value_bias": value_bias, "out_weight": out_weight, "out_bias": out_bias, "ln2_gain": ln2_gain, "ln2_bias": ln2_bias, "up_weight": up_weight, "up_bias": up_bias, "down_weight": down_weight, "down_bias": down_bias, "cotangent": cotangent}


@jax.custom_vjp
def low(v):
    return lax.optimization_barrier(v.astype(jnp.bfloat16)).astype(jnp.float32)

@jax.custom_vjp
def low_back(v):
    return v

def low_keep(v):
    return (low(v), None)

def low_pass(kept, grad):
    return (grad,)

def back_keep(v):
    return (v, None)

def back_low(kept, grad):
    return (low(grad),)
low.defvjp(low_keep, low_pass)
low_back.defvjp(back_keep, back_low)
epsilon = 1e-05
gelu_coeff = 0.7978845608028654

def precise(operand, matrix):
    return jnp.dot(operand, matrix, precision=lax.Precision.HIGHEST, preferred_element_type=jnp.float32)

def norm_rows(values, gain_vec, shift_vec):
    row_mean = lax.optimization_barrier(jnp.mean(values, axis=-1, keepdims=True))
    centred = values - row_mean
    row_var = lax.optimization_barrier(jnp.mean(centred * centred, axis=-1, keepdims=True))
    return centred * lax.rsqrt(row_var + epsilon) * gain_vec + shift_vec

def gelu_tanh(values):
    return 0.5 * values * (1.0 + jnp.tanh(gelu_coeff * (values + 0.044715 * values * values * values)))

def attend_head(triple, allowed):
    query_h, key_h, value_h = triple
    scores = low_back(precise(query_h, key_h.T) * HEAD_DIM ** (-0.5))
    scores = jnp.where(allowed, scores, -1e+30)
    weights_h = jax.nn.softmax(scores, axis=-1)
    return precise(low(weights_h), value_h)

def one_layer(state, params, allowed):
    gain_first, shift_first, w_mix, bias_query, bias_value, w_proj, bias_proj, gain_second, shift_second, w_upper, bias_upper, w_lower, bias_lower = params
    length = state.shape[0]
    width = state.shape[1]
    heads_count = width // HEAD_DIM
    normed = low(norm_rows(state, gain_first, shift_first))
    bias_all = jnp.concatenate([bias_query, jnp.zeros_like(bias_query), bias_value])
    mixed = low_back(low(precise(normed, w_mix) + bias_all))

    def split_heads(block):
        return block.reshape(length, heads_count, HEAD_DIM).transpose(1, 0, 2)
    query = split_heads(mixed[:, :width])
    key_part = split_heads(mixed[:, width:2 * width])
    value_part = split_heads(mixed[:, 2 * width:])
    attend = jax.checkpoint(attend_head)
    attended = lax.map(lambda triple: attend(triple, allowed), (query, key_part, value_part))
    attended = low_back(low(attended.transpose(1, 0, 2).reshape(length, width)))
    after_attn = state + low_back(precise(attended, w_proj) + bias_proj)
    normed_two = low(norm_rows(after_attn, gain_second, shift_second))
    hidden_in = low_back(precise(normed_two, w_upper) + bias_upper)
    hidden = low(gelu_tanh(hidden_in))
    return after_attn + low_back(precise(hidden, w_lower) + bias_lower)

def per_sequence(sequence, weight_sets, allowed):
    state = sequence
    for layer_index in range(LAYERS):
        state = one_layer(state, tuple((weight_stack[layer_index] for weight_stack in weight_sets)), allowed)
    return state

def reference(inputs, block_table, ln1_gain, ln1_bias, qkv_weight, query_bias, value_bias, out_weight, out_bias, ln2_gain, ln2_bias, up_weight, up_bias, down_weight, down_bias, cotangent):
    params = tuple((param.astype(jnp.float32) for param in (ln1_gain, ln1_bias, qkv_weight, query_bias, value_bias, out_weight, out_bias, ln2_gain, ln2_bias, up_weight, up_bias, down_weight, down_bias)))
    offsets = jnp.arange(BLK, dtype=jnp.int32)
    positions = (block_table.reshape(-1)[:, None] * BLK + offsets[None, :]).reshape(-1)
    allowed = positions[:, None] >= positions[None, :]
    saved = jax.checkpoint(per_sequence)

    def forward(sequences, weight_sets):
        return lax.map(lambda sequence: saved(sequence, weight_sets, allowed), sequences)
    result, pullback = jax.vjp(forward, inputs.astype(jnp.float32), params)
    grad_inputs, grad_params = pullback(cotangent.astype(jnp.float32))
    return (result.astype(jnp.bfloat16), grad_inputs, grad_params[0], grad_params[1], grad_params[2], grad_params[3], grad_params[4], grad_params[5], grad_params[6], grad_params[7], grad_params[8], grad_params[9], grad_params[10], grad_params[11], grad_params[12])
```

```python
import functools

import jax
import jax.numpy as jnp
from jax import lax
from jax.experimental import pallas as pl
from jax.experimental.pallas import tpu as pltpu
from jax.sharding import PartitionSpec as P

HEAD_DIM = 64
LAYERS = 2
GROUPS = 4

epsilon = 1e-05
gelu_coeff = 0.7978845608028654
BF = jnp.bfloat16
F32 = jnp.float32


def gelu_tanh(values):
    return (
        0.5 * values * (1.0 + jnp.tanh(gelu_coeff * (values + 0.044715 * values * values * values)))
    )


def dot_nt(a, b):
    return lax.dot_general(a, b, (((1,), (1,)), ((), ())), preferred_element_type=F32)


def dot_nn(a, b):
    return lax.dot_general(a, b, (((1,), (0,)), ((), ())), preferred_element_type=F32)


def dot_tn(a, b):
    return lax.dot_general(a, b, (((0,), (0,)), ((), ())), preferred_element_type=F32)


def whole(shape):
    return pl.BlockSpec(shape, lambda *_: (0,) * len(shape))


def norm_parts(values):
    mean = jnp.mean(values, axis=-1, keepdims=True)
    centred = values - mean
    var = jnp.mean(centred * centred, axis=-1, keepdims=True)
    scale = lax.rsqrt(var + epsilon)
    return centred * scale, scale


def norm_back(grad, unit, scale, gain):
    inner = grad * gain
    a = jnp.mean(inner, axis=-1, keepdims=True)
    b = jnp.mean(inner * unit, axis=-1, keepdims=True)
    return (
        scale * (inner - a - unit * b),
        jnp.sum(grad * unit, axis=0, keepdims=True),
        jnp.sum(grad, axis=0, keepdims=True),
    )


def split_refs(refs, *counts):
    out, at = [], 0
    for count in counts:
        out.append(refs[at : at + count])
        at += count
    return out


def mix_kernel(qkv_rows, group_ids, state_ref, gain_ref, shift_ref, w_ref, bias_ref, *refs):
    out_refs, (normed_ref, proj_ref) = split_refs(refs, GROUPS, 2)
    inner = w_ref.shape[0] // GROUPS
    unit, _ = norm_parts(state_ref[...])
    normed = (unit * gain_ref[...] + shift_ref[...]).astype(BF)
    normed_ref[...] = normed
    for k in range(GROUPS):
        g = group_ids[k]
        w = jnp.concatenate([w_ref[g * inner + e, :qkv_rows, :] for e in range(inner)], 0)
        out_refs[k][...] = (dot_nt(normed, w) + bias_ref[g]).astype(BF)
    proj = jnp.concatenate([w_ref[c, qkv_rows:, :] for c in range(w_ref.shape[0])], 0)
    proj = proj.astype(F32).T.astype(BF)
    gw = proj_ref.shape[1]
    for g in range(GROUPS):
        proj_ref[g] = proj[g * gw : (g + 1) * gw]


def mix(group_ids, state, gain, shift, w, bias):
    rows, width = state.shape
    cols = bias.shape[2]
    inner = w.shape[0] // GROUPS
    return pl.pallas_call(
        functools.partial(mix_kernel, cols // inner),
        out_shape=[jax.ShapeDtypeStruct((rows, cols), BF)] * GROUPS
        + [
            jax.ShapeDtypeStruct((rows, width), BF),
            jax.ShapeDtypeStruct((GROUPS, width // GROUPS, width), BF),
        ],
        grid_spec=pltpu.PrefetchScalarGridSpec(
            num_scalar_prefetch=1,
            grid=(1,),
            in_specs=[whole(state.shape), whole(gain.shape), whole(shift.shape), whole(w.shape), whole(bias.shape)],
            out_specs=[whole((rows, cols))] * GROUPS
            + [whole((rows, width)), whole((GROUPS, width // GROUPS, width))],
        ),
        compiler_params=pltpu.CompilerParams(vmem_limit_bytes=40 << 20),
        cost_estimate=pl.CostEstimate(
            flops=2 * rows * width * cols * GROUPS, bytes_accessed=2 * w.size, transcendentals=0
        ),
        name="mix",
    )(group_ids, state, gain, shift, w, bias)


def mix_back_kernel(
    qkv_rows, group_ids, grad_ref, state_ref, gain_ref, normed_ref, w_ref, dproj_ref, *refs
):
    gm_refs, (dw_ref, out_ref, dgain_ref, dshift_ref, dbias_ref) = split_refs(refs, GROUPS, 5)
    inner = w_ref.shape[0] // GROUPS
    rows = state_ref.shape[0]
    normed = normed_ref[...]
    ones = jnp.ones((8, rows), BF)
    total = None
    for k in range(GROUPS):
        g = group_ids[k]
        gm = gm_refs[k][...]
        w = jnp.concatenate([w_ref[g * inner + e, :qkv_rows, :] for e in range(inner)], 0)
        part = dot_nn(gm, w)
        total = part if total is None else total + part
        dw = dot_tn(gm, normed).astype(BF)
        for e in range(inner):
            dw_ref[g * inner + e, :qkv_rows, :] = dw[e * qkv_rows : (e + 1) * qkv_rows]
        dbias_ref[g] = dot_nn(ones, gm)
    dproj = jnp.concatenate([dproj_ref[g] for g in range(GROUPS)], 0)
    dproj = dproj.astype(F32).T.astype(BF)
    part = dproj.shape[0] // dw_ref.shape[0]
    for c in range(dw_ref.shape[0]):
        dw_ref[c, qkv_rows:, :] = dproj[c * part : (c + 1) * part]
    unit, scale = norm_parts(state_ref[...])
    back, dgain, dshift = norm_back(total, unit, scale, gain_ref[...])
    out_ref[...] = grad_ref[...] + back
    dgain_ref[...] = dgain
    dshift_ref[...] = dshift


def mix_back(group_ids, grad_after, state, gain, normed, w, dproj, gms):
    rows, width = state.shape
    cols = gms[0].shape[1]
    n = w.shape[0]
    inner = n // GROUPS
    vec = jax.ShapeDtypeStruct((1, width), F32)
    return pl.pallas_call(
        functools.partial(mix_back_kernel, cols // inner),
        out_shape=[
            jax.ShapeDtypeStruct(w.shape, BF),
            jax.ShapeDtypeStruct((rows, width), F32),
            vec,
            vec,
            jax.ShapeDtypeStruct((GROUPS, 8, cols), F32),
        ],
        grid_spec=pltpu.PrefetchScalarGridSpec(
            num_scalar_prefetch=1,
            grid=(1,),
            in_specs=[whole(x.shape) for x in (grad_after, state, gain, normed, w, dproj, *gms)],
            out_specs=[
                whole(w.shape),
                whole((rows, width)),
                whole((1, width)),
                whole((1, width)),
                whole((GROUPS, 8, cols)),
            ],
        ),
        compiler_params=pltpu.CompilerParams(vmem_limit_bytes=52 << 20),
        cost_estimate=pl.CostEstimate(
            flops=4 * rows * width * cols * GROUPS, bytes_accessed=4 * w.size, transcendentals=0
        ),
        name="mix_back",
    )(group_ids, grad_after, state, gain, normed, w, dproj, *gms)


def turn_weights_kernel(got_ref, attn_ref, feed_ref):
    m = got_ref.shape[0]
    attn_rows, width = attn_ref.shape
    part = width // m
    turned = jnp.concatenate([got_ref[i, :part, :] for i in range(m)], 0)
    turned = turned.astype(F32).T.astype(BF)
    attn_ref[...] = turned[:attn_rows]
    up = feed_ref.shape[0] // 2
    feed_ref[:up, :] = turned[attn_rows : attn_rows + up]
    down = up // m
    for i in range(m):
        feed_ref[up + i * down : up + (i + 1) * down, :] = got_ref[i, part : part + down, :]


def turn_feed_kernel(part_ref, out_ref):
    m, _, cols = out_ref.shape
    two, width = part_ref.shape
    rows, down = width // m, two // (2 * m)
    up = part_ref[: two // 2, :].astype(F32).T.astype(BF)
    for i in range(m):
        out_ref[i, :rows, :] = up[i * rows : (i + 1) * rows]
        low = part_ref[two // 2 + i * down : two // 2 + (i + 1) * down, :]
        for c in range(width // cols):
            out_ref[i, rows + c * down : rows + (c + 1) * down, :] = low[:, c * cols : (c + 1) * cols]


def turn_attn_kernel(part_ref, out_ref):
    m, rows, _ = out_ref.shape
    turned = part_ref[...].astype(F32).T.astype(BF)
    for i in range(m):
        out_ref[i] = turned[i * rows : (i + 1) * rows]


def turn(kernel, x, *shapes):
    out = [jax.ShapeDtypeStruct(shape, BF) for shape in shapes]
    return pl.pallas_call(
        kernel,
        out_shape=out if len(out) > 1 else out[0],
        compiler_params=pltpu.CompilerParams(vmem_limit_bytes=24 << 20),
        cost_estimate=pl.CostEstimate(flops=0, bytes_accessed=4 * x.size, transcendentals=0),
        name="turn",
    )(x)


def mlp_kernel(group_ids, state_ref, proj_ref, bproj_ref, gain_ref, shift_ref, w_ref, bup_ref, bdown_ref, *refs):
    att_refs, (after_ref, normed_ref, out_ref) = split_refs(refs, GROUPS, 3)
    c = pl.program_id(0)

    @pl.when(c == 0)
    def _():
        after = state_ref[...] + bproj_ref[...]
        for k in range(GROUPS):
            after = after + dot_nn(att_refs[k][...], proj_ref[group_ids[k]])
        after_ref[...] = after
        unit, _ = norm_parts(after)
        normed_ref[...] = (unit * gain_ref[...] + shift_ref[...]).astype(BF)
        out_ref[...] = after + bdown_ref[...]

    part = w_ref.shape[1] // 2
    hidden = gelu_tanh(dot_nt(normed_ref[...], w_ref[0, :part, :]) + bup_ref[0])
    out_ref[...] += dot_nn(hidden.astype(BF), w_ref[0, part:, :])


def mlp(group_ids, state, proj, bproj, gain, shift, w, bup, bdown, atts):
    rows, width = state.shape
    n, two, _ = w.shape
    wide = jax.ShapeDtypeStruct((rows, width), F32)
    return pl.pallas_call(
        mlp_kernel,
        out_shape=[wide, jax.ShapeDtypeStruct((rows, width), BF), wide],
        grid_spec=pltpu.PrefetchScalarGridSpec(
            num_scalar_prefetch=1,
            grid=(n,),
            in_specs=[whole(x.shape) for x in (state, proj, bproj, gain, shift)]
            + [
                pl.BlockSpec((1, two, width), lambda c, *_: (c, 0, 0)),
                pl.BlockSpec((1, 1, two // 2), lambda c, *_: (c, 0, 0)),
                whole(bdown.shape),
            ]
            + [whole(x.shape) for x in atts],
            out_specs=[whole((rows, width))] * 3,
        ),
        compiler_params=pltpu.CompilerParams(vmem_limit_bytes=40 << 20),
        cost_estimate=pl.CostEstimate(
            flops=2 * rows * (w.size + proj.size), bytes_accessed=2 * w.size, transcendentals=0
        ),
        name="mlp",
    )(group_ids, state, proj, bproj, gain, shift, w, bup, bdown, *atts)


def mlp_back_kernel(
    group_ids, grad_ref, after_ref, normed_ref, gain_ref, proj_ref, w_ref, bup_ref, *refs
):
    att_refs, datt_refs, outs, (dx_ref,) = split_refs(refs, GROUPS, GROUPS, 8, 1)
    dw_ref, dproj_ref, gafter_ref, dgain_ref, dshift_ref, dbup_ref, dbdown_ref, dbproj_ref = outs
    c = pl.program_id(0)
    rows, width = grad_ref.shape
    part = w_ref.shape[1] // 2
    grad = grad_ref[...].astype(BF)
    normed = normed_ref[...]
    up, down = w_ref[0, :part, :], w_ref[0, part:, :]
    bias = jnp.broadcast_to(bup_ref[0], (8, part)).T[:, :1]

    @pl.when(c == 0)
    def _():
        dx_ref[...] = jnp.zeros_like(dx_ref)
        dbdown_ref[...] = jnp.sum(grad.astype(F32), axis=0, keepdims=True)

    hid = dot_nt(up, normed) + bias
    square = hid * hid
    th = jnp.tanh(gelu_coeff * (hid + 0.044715 * hid * square))
    value = (0.5 * hid * (1.0 + th)).astype(BF)
    slope = 0.5 * (1.0 + th) + 0.5 * hid * (1.0 - th * th) * gelu_coeff * (
        1.0 + 3 * 0.044715 * square
    )
    ghid = (dot_nt(down, grad) * slope).astype(BF)
    dbup_ref[0] = dot_nt(jnp.ones((8, rows), BF), ghid)
    dw_ref[0, :part, :] = dot_nn(ghid, normed).astype(BF)
    dw_ref[0, part:, :] = dot_nn(value, grad).astype(BF)
    dx_ref[...] += dot_tn(ghid, up)

    @pl.when(c == pl.num_programs(0) - 1)
    def _():
        unit, scale = norm_parts(after_ref[...])
        back, dgain, dshift = norm_back(dx_ref[...], unit, scale, gain_ref[...])
        gafter = grad_ref[...] + back
        gafter_ref[...] = gafter
        dgain_ref[...] = dgain
        dshift_ref[...] = dshift
        gatt = gafter.astype(BF)
        dbproj_ref[...] = jnp.sum(gatt.astype(F32), axis=0, keepdims=True)
        for k in range(GROUPS):
            g = group_ids[k]
            datt_refs[k][...] = dot_nt(gatt, proj_ref[g]).astype(BF)
            dproj_ref[g] = dot_tn(att_refs[k][...], gatt).astype(BF)


def mlp_back(group_ids, grad, after, normed, gain, proj, w, bup, atts):
    rows, width = grad.shape
    n, two, _ = w.shape
    gw = width // GROUPS
    vec = jax.ShapeDtypeStruct((1, width), F32)
    step_w = pl.BlockSpec((1, two, width), lambda c, *_: (c, 0, 0))
    return pl.pallas_call(
        mlp_back_kernel,
        out_shape=[jax.ShapeDtypeStruct((rows, gw), BF)] * GROUPS
        + [
            jax.ShapeDtypeStruct(w.shape, BF),
            jax.ShapeDtypeStruct(proj.shape, BF),
            jax.ShapeDtypeStruct((rows, width), F32),
            vec,
            vec,
            jax.ShapeDtypeStruct((n, 8, two // 2), F32),
            vec,
            vec,
        ],
        grid_spec=pltpu.PrefetchScalarGridSpec(
            num_scalar_prefetch=1,
            grid=(n,),
            in_specs=[whole(x.shape) for x in (grad, after, normed, gain, proj)]
            + [step_w, pl.BlockSpec((1, 1, two // 2), lambda c, *_: (c, 0, 0))]
            + [whole(x.shape) for x in atts],
            out_specs=[whole((rows, gw))] * GROUPS
            + [
                step_w,
                whole(proj.shape),
                whole((rows, width)),
                whole((1, width)),
                whole((1, width)),
                pl.BlockSpec((1, 8, two // 2), lambda c, *_: (c, 0, 0)),
                whole((1, width)),
                whole((1, width)),
            ],
            scratch_shapes=[pltpu.VMEM((rows, width), F32)],
        ),
        compiler_params=pltpu.CompilerParams(vmem_limit_bytes=48 << 20),
        cost_estimate=pl.CostEstimate(
            flops=5 * rows * w.size + 4 * rows * proj.size, bytes_accessed=4 * w.size, transcendentals=0
        ),
        name="mlp_back",
    )(group_ids, grad, after, normed, gain, proj, w, bup, *atts)


def head_masks(rows, width):
    lane = lax.broadcasted_iota(jnp.int32, (rows, width), 1)
    return [
        (lane >= h * HEAD_DIM) & (lane < (h + 1) * HEAD_DIM) for h in range(width // HEAD_DIM)
    ]


def only_head(block, masks):
    wide = block.astype(F32)
    return [jnp.where(mask, wide, 0.0).astype(BF) for mask in masks]


def causal_tile(blk):
    key_at = lax.broadcasted_iota(jnp.int32, (blk, blk), 0)
    query_at = lax.broadcasted_iota(jnp.int32, (blk, blk), 1)
    return key_at <= query_at


def query_part(ref, rows, width):
    low = width // 128 * 128
    high = -(-2 * width // 128) * 128
    window = ref[rows, low:high].astype(F32)
    if width > low:
        window = pltpu.roll(window, high - width, 1)
    return (window[:, :width] * (HEAD_DIM ** (-0.5))).astype(BF)


def attend_kernel(q_id, k_loc, *refs):
    mixed_refs, o_refs, (lse_ref, q_ref, k_ref, vt_ref, acc_ref) = split_refs(
        refs, len(refs) - GROUPS - 5, GROUPS, 5
    )
    q_blocks, blk, width = q_ref.shape
    heads = width // HEAD_DIM

    for r, ref in enumerate(mixed_refs):
        for b in range(2):
            rows = slice(b * blk, (b + 1) * blk)
            k_ref[2 * r + b] = ref[rows, :width]
            vt_ref[2 * r + b] = ref[rows, 2 * width :].astype(F32).T.astype(BF)
            if r < GROUPS:
                q_ref[2 * r + b] = query_part(ref, rows, width)
    masks = head_masks(blk, width)

    def per_query(qb):
        q_blk = q_ref[qb]
        q_h = only_head(q_blk, masks)
        own = q_id[qb]
        loc = k_loc[own]
        keys = k_ref[loc]
        tri = causal_tile(blk)
        stats = []
        for h in range(heads):
            rows = slice(h * HEAD_DIM, (h + 1) * HEAD_DIM)
            s = jnp.where(tri, dot_nt(keys, q_h[h]), -1e30)
            top = jnp.max(s, axis=0, keepdims=True)
            p = jnp.exp(s - top)
            stats.append((top, jnp.sum(p, axis=0, keepdims=True)))
            acc_ref[rows, :] = dot_nn(vt_ref[loc, rows, :], p.astype(BF))

        def step(i, carry):
            loc = k_loc[i]
            keys = k_ref[loc]
            out = []
            for h in range(heads):
                rows = slice(h * HEAD_DIM, (h + 1) * HEAD_DIM)
                top, total = carry[h]
                s = dot_nt(keys, q_h[h])
                new = jnp.maximum(top, jnp.max(s, axis=0, keepdims=True))
                alpha = jnp.exp(top - new)
                p = jnp.exp(s - new)
                out.append((new, total * alpha + jnp.sum(p, axis=0, keepdims=True)))
                acc_ref[rows, :] = acc_ref[rows, :] * alpha + dot_nn(
                    vt_ref[loc, rows, :], p.astype(BF)
                )
            return tuple(out)

        stats = lax.fori_loop(0, own, step, tuple(stats))
        for h in range(heads):
            rows = slice(h * HEAD_DIM, (h + 1) * HEAD_DIM)
            top, total = stats[h]
            acc_ref[rows, :] = acc_ref[rows, :] / total
            lse_ref[qb, h : h + 1, :] = top + jnp.log(total)
        return acc_ref[...].T.astype(BF)

    for k in range(GROUPS):

        def pair(b, _, k=k):
            start = pl.multiple_of(b * blk, 32)
            o_refs[k][pl.ds(start, blk), :] = per_query(2 * k + b)
            return 0

        lax.fori_loop(0, 2, pair, 0)


def attend(q_id, k_loc, mixed):
    rows, cols = mixed[0].shape
    blk, width = rows // 2, cols // 3
    q_blocks, k_blocks = 2 * GROUPS, 2 * len(mixed)
    return pl.pallas_call(
        attend_kernel,
        out_shape=[jax.ShapeDtypeStruct((rows, width), BF)] * GROUPS
        + [jax.ShapeDtypeStruct((q_blocks, 8, blk), F32)],
        grid_spec=pltpu.PrefetchScalarGridSpec(
            num_scalar_prefetch=2,
            grid=(1,),
            in_specs=[whole(x.shape) for x in mixed],
            out_specs=[whole((rows, width))] * GROUPS + [whole((q_blocks, 8, blk))],
            scratch_shapes=[
                pltpu.VMEM((q_blocks, blk, width), BF),
                pltpu.VMEM((k_blocks, blk, width), BF),
                pltpu.VMEM((k_blocks, width, blk), BF),
                pltpu.VMEM((width, blk), F32),
            ],
        ),
        compiler_params=pltpu.CompilerParams(vmem_limit_bytes=48 << 20),
        cost_estimate=pl.CostEstimate(
            flops=4 * q_blocks * k_blocks * blk * blk * width,
            bytes_accessed=2 * len(mixed) * rows * cols,
            transcendentals=q_blocks * k_blocks * blk * blk * 2,
        ),
        name="attend",
    )(q_id, k_loc, *mixed)


def attend_back_kernel(q_id, k_loc, *refs):
    count = (len(refs) - 2 * GROUPS - 9) // 2
    mixed_refs, o_refs, do_refs, (lse_ref,), dm_refs, scratch = split_refs(
        refs, count, GROUPS, GROUPS, 1, count, 8
    )
    q_ref, k_ref, v_ref, kt_ref, dq_ref, dka_ref, dva_ref, dqt_ref = scratch
    q_blocks, blk, width = q_ref.shape
    heads = width // HEAD_DIM
    for r, ref in enumerate(mixed_refs):
        for b in range(2):
            rows = slice(b * blk, (b + 1) * blk)
            at = 2 * r + b
            keys = ref[rows, :width]
            k_ref[at] = keys
            kt_ref[at] = keys.astype(F32).T.astype(BF)
            v_ref[at] = ref[rows, 2 * width :]
            if r < GROUPS:
                q_ref[at] = query_part(ref, rows, width)

    def clear(b, _):
        dka_ref[b] = jnp.zeros((blk, width), F32)
        dva_ref[b] = jnp.zeros((blk, width), F32)
        return 0

    lax.fori_loop(0, k_ref.shape[0], clear, 0)
    masks = head_masks(blk, width)

    def per_query(qb, do_blk, o_blk):
        q_blk = q_ref[qb]
        q_h = only_head(q_blk, masks)
        do_h = only_head(do_blk, masks)
        both = (do_blk.astype(F32) * o_blk.astype(F32)).T
        delta = [
            jnp.sum(both[h * HEAD_DIM : (h + 1) * HEAD_DIM], axis=0, keepdims=True)
            for h in range(heads)
        ]
        lse = [lse_ref[qb, h : h + 1, :] for h in range(heads)]
        own = q_id[qb]

        def tile(loc, tri, first):
            keys = k_ref[loc]
            values = v_ref[loc]
            dk = dka_ref[loc]
            dv = dva_ref[loc]
            for h in range(heads):
                rows = slice(h * HEAD_DIM, (h + 1) * HEAD_DIM)
                p = jnp.exp(dot_nt(keys, q_h[h]) - lse[h])
                if tri is not None:
                    p = jnp.where(tri, p, 0.0)
                dp = dot_nt(values, do_h[h])
                ds = (p * (dp - delta[h])).astype(BF)
                dv = dv + dot_nn(p.astype(BF), do_h[h])
                dk = dk + dot_nn(ds, q_h[h])
                dq = dot_nn(kt_ref[loc, rows, :], ds)
                dqt_ref[rows, :] = dq if first else dqt_ref[rows, :] + dq
            dka_ref[loc] = dk
            dva_ref[loc] = dv

        tile(k_loc[own], causal_tile(blk), True)

        def step(i, _):
            tile(k_loc[i], None, False)
            return 0

        lax.fori_loop(0, own, step, 0)
        dq_ref[qb] = (dqt_ref[...] * (HEAD_DIM ** (-0.5))).T

    for k in range(GROUPS):

        def pair(b, _, k=k):
            rows = pl.ds(pl.multiple_of(b * blk, 32), blk)
            per_query(2 * k + b, do_refs[k][rows, :], o_refs[k][rows, :])
            return 0

        lax.fori_loop(0, 2, pair, 0)

    for r, ref in enumerate(dm_refs):

        def finish(b, _, r=r, ref=ref):
            at = 2 * r + b
            dq = dq_ref[at] if r < GROUPS else jnp.zeros((blk, width), F32)
            joined = jnp.concatenate([dka_ref[at], dq, dva_ref[at]], 1)
            ref[pl.ds(pl.multiple_of(b * blk, 32), blk), :] = joined.astype(BF)
            return 0

        lax.fori_loop(0, 2, finish, 0)


def attend_back(q_id, k_loc, mixed, o, do, lse):
    rows, cols = mixed[0].shape
    blk, width = rows // 2, cols // 3
    q_blocks, k_blocks = 2 * GROUPS, 2 * len(mixed)
    return pl.pallas_call(
        attend_back_kernel,
        out_shape=[jax.ShapeDtypeStruct((rows, cols), BF)] * len(mixed),
        grid_spec=pltpu.PrefetchScalarGridSpec(
            num_scalar_prefetch=2,
            grid=(1,),
            in_specs=[whole(x.shape) for x in (*mixed, *o, *do, lse)],
            out_specs=[whole((rows, cols))] * len(mixed),
            scratch_shapes=[
                pltpu.VMEM((q_blocks, blk, width), BF),
                pltpu.VMEM((k_blocks, blk, width), BF),
                pltpu.VMEM((k_blocks, blk, width), BF),
                pltpu.VMEM((k_blocks, width, blk), BF),
                pltpu.VMEM((q_blocks, blk, width), F32),
                pltpu.VMEM((k_blocks, blk, width), F32),
                pltpu.VMEM((k_blocks, blk, width), F32),
                pltpu.VMEM((width, blk), F32),
            ],
        ),
        compiler_params=pltpu.CompilerParams(vmem_limit_bytes=56 << 20),
        cost_estimate=pl.CostEstimate(
            flops=10 * q_blocks * k_blocks * blk * blk * width,
            bytes_accessed=4 * len(mixed) * rows * cols,
            transcendentals=q_blocks * k_blocks * blk * blk * 2,
        ),
        name="attend_back",
    )(q_id, k_loc, *mixed, *o, *do, lse)


def swap(x, axis_name, size, k):
    return lax.ppermute(x, axis_name, [(i, i ^ k) for i in range(size)])


def pick(x, at):
    return lax.dynamic_index_in_dim(x, at, 0, keepdims=False)


class Place:
    def __init__(self, n, m):
        self.n, self.m = n, m
        self.inner = n // GROUPS
        self.idx = lax.axis_index("ctx")
        self.outer_at = self.idx // self.inner
        self.inner_at = self.idx % self.inner
        self.w = lax.axis_index("wt")

    def exchange(self, parts):
        return [parts[0]] + [
            swap(parts[k], "ctx", self.n, k * self.inner) for k in range(1, GROUPS)
        ]

    def scatter_ctx(self, x):
        return lax.psum_scatter(x, "ctx", scatter_dimension=0, tiled=True)

    def gather_ctx(self, x):
        return lax.all_gather(x, "ctx", axis=0, tiled=False)

    def scatter_wt(self, x):
        total = pick(x, self.w).astype(F32)
        for k in range(1, self.m):
            total = total + swap(pick(x, self.w ^ k), "wt", self.m, k).astype(F32)
        return total

    def total(self, x):
        for axis_name, size in (("ctx", self.n), ("wt", self.m)):
            k = 1
            while k < size:
                x = x + swap(x, axis_name, size, k)
                k *= 2
        return x


def split_columns(shard, at, count, groups):
    rows, cols = shard.shape
    c = cols // (groups * count)
    cut = shard.reshape(rows, groups, count, c)
    return lax.dynamic_index_in_dim(cut, at, 2, keepdims=False).reshape(rows, groups * c)


def qkv_piece(shard, place):
    rows, cols = shard.shape
    cut = shard.reshape(rows, 3, GROUPS, cols // (3 * GROUPS))
    own = lax.dynamic_index_in_dim(cut, place.outer_at, 2, keepdims=False)
    own = jnp.concatenate([own[:, 1], own[:, 0], own[:, 2]], 1)
    part = own.shape[1] // place.inner
    return lax.dynamic_slice_in_dim(own, place.inner_at * part, part, 1)


def after(x, done):
    return lax.optimization_barrier((x, done))[0]


def pack_layer(place, matrices, layer):
    qkv_weight, out_weight, up_weight, down_weight = matrices
    n, m = place.n, place.m
    width, ff = out_weight.shape[2], up_weight.shape[2]
    columns = jnp.concatenate(
        [
            qkv_piece(qkv_weight[layer], place),
            split_columns(out_weight[layer], place.idx, n, 1),
            split_columns(up_weight[layer], place.idx, n, m),
        ],
        1,
    )
    pad = -columns.shape[1] % width
    assert pad == 0 or columns.shape[1] < width
    if pad:
        columns = jnp.pad(columns, ((0, 0), (0, pad)))
    down = pick(down_weight[layer].reshape(n, ff // (n * m), width), place.idx)
    return jnp.concatenate([columns, down], 0)


def pack_small(small, width):
    flat = [s.reshape(-1) for s in small]
    size = sum(f.shape[0] for f in flat)
    extra = -(-size // (width * 16)) * 16
    flat.append(jnp.zeros((extra * width - size,), BF))
    return jnp.concatenate(flat).reshape(extra, width)


def unpack_small(place, got, small):
    got = got.reshape(place.m, -1)
    out, at = [], 0
    for s in small:
        count, c = s.shape
        part = got[:, at : at + count * c].reshape(place.m, count, c)
        out.append(part.transpose(1, 0, 2).reshape(count, place.m * c).astype(F32))
        at += count * c
    return out


def gather_layer(place, got, ff):
    width = got.shape[2]
    attn_rows = 4 * width // place.n
    attn, feed = turn(
        turn_weights_kernel, got, (attn_rows, width), (2 * ff // place.n, width)
    )
    attn = place.gather_ctx(attn)
    return attn, place.gather_ctx(after(feed, attn))


def scatter_part(place, dw, ready, kernel, rows):
    n, two, width = dw.shape
    dw = dw.reshape(n * two, width)
    if ready is not None:
        dw = after(dw, ready)
    part = place.scatter_ctx(dw)
    return turn(kernel, part, (place.m, rows, two * width // (place.m * rows)))


def unpack_feed(place, own, ff, width):
    n, m = place.n, place.m
    rows = width // m
    up, down = own[:, :rows], own[:, rows:]
    up = up.reshape(n, rows, m, ff // (n * m)).transpose(1, 2, 0, 3).reshape(rows, ff)
    down = down.reshape(n, -1, ff // (n * m), down.shape[2]).transpose(0, 2, 1, 3)
    return up.astype(F32), down.reshape(ff // m, width).astype(F32)


def unpack_both(place, joined, ff, width):
    cut = width // place.m
    return unpack_attn(place, joined[:, :cut], width) + unpack_feed(place, joined[:, cut:], ff, width)


def unpack_attn(place, own, width):
    n, m = place.n, place.m
    rows = 3 * width // n
    gw = width // GROUPS
    qkv, proj = own[:, :, :rows], own[:, :, rows:]
    qkv = qkv.reshape(GROUPS, place.inner, width // m, rows).transpose(2, 0, 1, 3)
    qkv = qkv.reshape(width // m, GROUPS, 3, gw)
    qkv = jnp.concatenate([qkv[:, :, i].reshape(width // m, width) for i in (1, 0, 2)], 1)
    proj = proj.transpose(1, 0, 2).reshape(width // m, width)
    return qkv.astype(F32), proj.astype(F32)


def reduce_small(place, smalls):
    sizes = [v.shape[0] for v in smalls[0]]
    packed = jnp.concatenate([v for layer in smalls for v in layer]).reshape(-1, 128)
    packed = place.total(packed).reshape(len(smalls), -1)
    out, at = [], 0
    for size in sizes:
        part = packed[:, at : at + size].reshape(len(smalls), place.m, size // place.m)
        out.append(lax.dynamic_index_in_dim(part, place.w, 1, keepdims=False))
        at += size
    return out


def body(
    n, m, inputs, block_table, ln1_gain, ln1_bias, qkv_weight, query_bias, value_bias, out_weight,
    out_bias, ln2_gain, ln2_bias, up_weight, up_bias, down_weight, down_bias, cotangent,
):
    place = Place(n, m)
    rows, width = inputs.shape[1:]
    ff = up_weight.shape[2]
    gw = width // GROUPS
    group_ids = jnp.stack([place.outer_at ^ k for k in range(GROUPS)]).astype(jnp.int32)
    key_ids = jnp.concatenate(
        [
            pick(block_table, place.idx ^ (k * place.inner + j))
            for j in range(place.inner)
            for k in range(GROUPS)
        ]
    ).astype(jnp.int32)
    q_id = key_ids[: 2 * GROUPS]
    at = jnp.arange(2 * n, dtype=jnp.int32)
    k_loc = jnp.sum(jnp.where(key_ids[None, :] == at[:, None], at[None, :], 0), axis=1).astype(jnp.int32)

    small = (ln1_gain, ln1_bias, query_bias, value_bias, out_bias, ln2_gain, ln2_bias, up_bias, down_bias)
    matrices = (qkv_weight, out_weight, up_weight, down_weight)
    first = jnp.concatenate([pack_layer(place, matrices, 0), pack_small(small, width)], 0)
    got = lax.all_gather(first, "wt", axis=0, tiled=False)
    big_rows = width // m + ff // (n * m)
    vectors = unpack_small(place, got[:, big_rows:], small)
    weights = [gather_layer(place, got, ff)]
    params = []
    for layer in range(LAYERS):
        v = [x[layer].reshape(1, -1) for x in vectors]
        bias = jnp.concatenate(
            [jnp.zeros((GROUPS, 1, gw), F32), v[2].reshape(GROUPS, 1, gw), v[3].reshape(GROUPS, 1, gw)], 2
        )
        bup = v[7].reshape(m, n, ff // (n * m)).transpose(1, 0, 2).reshape(n, 1, ff // n)
        params.append((v, bias, bup))

    state = inputs[0].astype(F32)
    saved = []
    for layer in range(LAYERS):
        attn, feed = weights[layer]
        v, bias, bup = params[layer]
        *mixed, normed, proj = mix(group_ids, state, v[0], v[1], attn, bias)
        mixed = place.exchange(mixed)
        if layer + 1 < LAYERS:
            send = after(pack_layer(place, matrices, layer + 1), mixed[1])
            coming = lax.all_gather(send, "wt", axis=0, tiled=False)
        mixed = mixed + [
            swap(x, "ctx", n, j) for j in range(1, place.inner) for x in mixed
        ]
        *o, lse = attend(q_id, k_loc, mixed)
        if layer + 1 < LAYERS:
            weights.append(gather_layer(place, after(coming, o[0]), ff))
        atts = place.exchange(o)
        mid, normed_two, new = mlp(
            group_ids, state, proj, v[4], v[5], v[6], feed, bup, v[8], atts
        )
        saved.append((state, normed, mixed, o, lse, atts, mid, normed_two, proj))
        state = new
    outputs = state.astype(BF)[None]
    gradient = cotangent[0].astype(F32)
    shards, smalls, ready = [None] * LAYERS, [None] * LAYERS, None
    for layer in reversed(range(LAYERS)):
        attn, feed = weights[layer]
        v, bias, bup = params[layer]
        before, normed, mixed, o, lse, atts, mid, normed_two, proj = saved[layer]
        *datts, dfeed, dproj, gafter, dgain2, dshift2, dbup, dbdown, dbproj = mlp_back(
            group_ids, gradient, mid, normed_two, v[5], proj, feed, bup, atts
        )
        part_feed = scatter_part(place, dfeed, ready, turn_feed_kernel, 2 * width // m)
        do = place.exchange(datts)
        dm = list(attend_back(q_id, k_loc, mixed, o, do, lse))
        dm[0] = after(dm[0], part_feed)
        own_feed = place.scatter_wt(part_feed).astype(BF)
        own = []
        for k in range(GROUPS):
            if place.inner == 1:
                own.append(dm[k])
                continue
            total = dm[k].astype(F32)
            for j in range(1, place.inner):
                total = total + swap(dm[j * GROUPS + k], "ctx", n, j).astype(F32)
            own.append(total.astype(BF))
        gms = place.exchange(own)
        dmix, gradient, dgain1, dshift1, dbias = mix_back(
            group_ids, gafter, before, v[0], normed, attn, dproj, gms
        )
        if layer + 1 < LAYERS:
            joined = place.gather_ctx(after(pending, part_feed))
            shards[layer + 1] = unpack_both(place, joined, ff, width)
            dmix = after(dmix, joined)
        part_attn = scatter_part(place, dmix, part_feed, turn_attn_kernel, width // m)
        own_attn = place.scatter_wt(part_attn).astype(BF)
        pending = jnp.concatenate([own_attn, own_feed], 0)
        ready = part_attn
        if layer == 0:
            own_feed = place.gather_ctx(own_feed)
            own_attn = place.gather_ctx(after(own_attn, own_feed))
            shards[layer] = unpack_attn(place, own_attn, width) + unpack_feed(place, own_feed, ff, width)
        dbup = dbup[:, 0].reshape(n, m, ff // (n * m)).transpose(1, 0, 2)
        smalls[layer] = [
            x.reshape(-1)
            for x in (
                dgain1, dshift1, dbias[:, 0, gw : 2 * gw], dbias[:, 0, 2 * gw :], dbproj,
                dgain2, dshift2, dbup, dbdown,
            )
        ]
    vec = reduce_small(place, smalls)
    mixw, projw, up, down = [jnp.stack([s[i] for s in shards]) for i in range(4)]
    return (
        outputs, gradient[None], vec[0], vec[1], mixw, vec[2], vec[3], projw, vec[4],
        vec[5], vec[6], up, vec[7], down, vec[8],
    )


def solution(mesh):
    row, vec, mat = P("wt", "ctx", None), P(None, "wt"), P(None, "wt", None)
    in_specs = (row, P(), vec, vec, mat, vec, vec, mat, vec, vec, vec, mat, vec, mat, vec, row)
    out_specs = (row, row, vec, vec, mat, vec, vec, mat, vec, vec, vec, mat, vec, mat, vec)
    return jax.shard_map(
        functools.partial(body, mesh.shape["ctx"], mesh.shape["wt"]),
        mesh=mesh,
        in_specs=in_specs,
        out_specs=out_specs,
        check_vma=False,
    )
```

```python
import functools

import jax
import jax.numpy as jnp
from jax import lax
from jax.experimental import pallas as pl
from jax.experimental.pallas import tpu as pltpu
from jax.sharding import PartitionSpec as P

HEAD_DIM = 64
LAYERS = 2
GROUPS = 4

epsilon = 1e-05
gelu_coeff = 0.7978845608028654
BF = jnp.bfloat16
F32 = jnp.float32


def gelu_tanh(values):
    return (
        0.5 * values * (1.0 + jnp.tanh(gelu_coeff * (values + 0.044715 * values * values * values)))
    )


def dot_nt(a, b):
    return lax.dot_general(a, b, (((1,), (1,)), ((), ())), preferred_element_type=F32)


def dot_nn(a, b):
    return lax.dot_general(a, b, (((1,), (0,)), ((), ())), preferred_element_type=F32)


def dot_tn(a, b):
    return lax.dot_general(a, b, (((0,), (0,)), ((), ())), preferred_element_type=F32)


def whole(shape):
    return pl.BlockSpec(shape, lambda *_: (0,) * len(shape))


def norm_parts(values):
    mean = jnp.mean(values, axis=-1, keepdims=True)
    centred = values - mean
    var = jnp.mean(centred * centred, axis=-1, keepdims=True)
    scale = lax.rsqrt(var + epsilon)
    return centred * scale, scale


def norm_back(grad, unit, scale, gain):
    inner = grad * gain
    a = jnp.mean(inner, axis=-1, keepdims=True)
    b = jnp.mean(inner * unit, axis=-1, keepdims=True)
    return (
        scale * (inner - a - unit * b),
        jnp.sum(grad * unit, axis=0, keepdims=True),
        jnp.sum(grad, axis=0, keepdims=True),
    )


def split_refs(refs, *counts):
    out, at = [], 0
    for count in counts:
        out.append(refs[at : at + count])
        at += count
    return out


def mix_kernel(qkv_rows, group_ids, state_ref, gain_ref, shift_ref, w_ref, bias_ref, *refs):
    out_refs, (normed_ref, proj_ref) = split_refs(refs, GROUPS, 2)
    inner = w_ref.shape[0] // GROUPS
    unit, _ = norm_parts(state_ref[...])
    normed = (unit * gain_ref[...] + shift_ref[...]).astype(BF)
    normed_ref[...] = normed
    for k in range(GROUPS):
        g = group_ids[k]
        w = jnp.concatenate([w_ref[g * inner + e, :qkv_rows, :] for e in range(inner)], 0)
        out_refs[k][...] = (dot_nt(normed, w) + bias_ref[g]).astype(BF)
    proj = jnp.concatenate([w_ref[c, qkv_rows:, :] for c in range(w_ref.shape[0])], 0)
    proj = proj.astype(F32).T.astype(BF)
    gw = proj_ref.shape[1]
    for g in range(GROUPS):
        proj_ref[g] = proj[g * gw : (g + 1) * gw]


def mix(group_ids, state, gain, shift, w, bias):
    rows, width = state.shape
    cols = bias.shape[2]
    inner = w.shape[0] // GROUPS
    return pl.pallas_call(
        functools.partial(mix_kernel, cols // inner),
        out_shape=[jax.ShapeDtypeStruct((rows, cols), BF)] * GROUPS
        + [
            jax.ShapeDtypeStruct((rows, width), BF),
            jax.ShapeDtypeStruct((GROUPS, width // GROUPS, width), BF),
        ],
        grid_spec=pltpu.PrefetchScalarGridSpec(
            num_scalar_prefetch=1,
            grid=(1,),
            in_specs=[whole(state.shape), whole(gain.shape), whole(shift.shape), whole(w.shape), whole(bias.shape)],
            out_specs=[whole((rows, cols))] * GROUPS
            + [whole((rows, width)), whole((GROUPS, width // GROUPS, width))],
        ),
        compiler_params=pltpu.CompilerParams(vmem_limit_bytes=40 << 20),
        cost_estimate=pl.CostEstimate(
            flops=2 * rows * width * cols * GROUPS, bytes_accessed=2 * w.size, transcendentals=0
        ),
        name="mix",
    )(group_ids, state, gain, shift, w, bias)


def mix_back_kernel(
    qkv_rows, group_ids, grad_ref, state_ref, gain_ref, normed_ref, w_ref, dproj_ref, *refs
):
    gm_refs, (dw_ref, out_ref, dgain_ref, dshift_ref, dbias_ref) = split_refs(refs, GROUPS, 5)
    inner = w_ref.shape[0] // GROUPS
    rows = state_ref.shape[0]
    normed = normed_ref[...]
    ones = jnp.ones((8, rows), BF)
    total = None
    for k in range(GROUPS):
        g = group_ids[k]
        gm = gm_refs[k][...]
        w = jnp.concatenate([w_ref[g * inner + e, :qkv_rows, :] for e in range(inner)], 0)
        part = dot_nn(gm, w)
        total = part if total is None else total + part
        dw = dot_tn(gm, normed).astype(BF)
        for e in range(inner):
            dw_ref[g * inner + e, :qkv_rows, :] = dw[e * qkv_rows : (e + 1) * qkv_rows]
        dbias_ref[g] = dot_nn(ones, gm)
    dproj = jnp.concatenate([dproj_ref[g] for g in range(GROUPS)], 0)
    dproj = dproj.astype(F32).T.astype(BF)
    part = dproj.shape[0] // dw_ref.shape[0]
    for c in range(dw_ref.shape[0]):
        dw_ref[c, qkv_rows:, :] = dproj[c * part : (c + 1) * part]
    unit, scale = norm_parts(state_ref[...])
    back, dgain, dshift = norm_back(total, unit, scale, gain_ref[...])
    out_ref[...] = grad_ref[...] + back
    dgain_ref[...] = dgain
    dshift_ref[...] = dshift


def mix_back(group_ids, grad_after, state, gain, normed, w, dproj, gms):
    rows, width = state.shape
    cols = gms[0].shape[1]
    n = w.shape[0]
    inner = n // GROUPS
    vec = jax.ShapeDtypeStruct((1, width), F32)
    return pl.pallas_call(
        functools.partial(mix_back_kernel, cols // inner),
        out_shape=[
            jax.ShapeDtypeStruct(w.shape, BF),
            jax.ShapeDtypeStruct((rows, width), F32),
            vec,
            vec,
            jax.ShapeDtypeStruct((GROUPS, 8, cols), F32),
        ],
        grid_spec=pltpu.PrefetchScalarGridSpec(
            num_scalar_prefetch=1,
            grid=(1,),
            in_specs=[whole(x.shape) for x in (grad_after, state, gain, normed, w, dproj, *gms)],
            out_specs=[
                whole(w.shape),
                whole((rows, width)),
                whole((1, width)),
                whole((1, width)),
                whole((GROUPS, 8, cols)),
            ],
        ),
        compiler_params=pltpu.CompilerParams(vmem_limit_bytes=52 << 20),
        cost_estimate=pl.CostEstimate(
            flops=12 * rows * width * cols * GROUPS, bytes_accessed=4 * w.size, transcendentals=0
        ),
        name="mix_back",
    )(group_ids, grad_after, state, gain, normed, w, dproj, *gms)


def turn_weights_kernel(w_at, *refs):
    parts, (attn_ref, feed_ref, rows_ref) = split_refs(refs, len(refs) - 3, 3)
    m = len(parts)
    attn_rows, width = attn_ref.shape
    part = width // m
    up = feed_ref.shape[0] // 2
    down = up // m
    for k, ref in enumerate(parts):
        rows_ref[w_at[0] ^ k] = ref[: part + down, :]
    turned = jnp.concatenate([rows_ref[i, :part, :] for i in range(m)], 0)
    turned = turned.astype(F32).T.astype(BF)
    attn_ref[...] = turned[:attn_rows]
    feed_ref[:up, :] = turned[attn_rows : attn_rows + up]
    for i in range(m):
        feed_ref[up + i * down : up + (i + 1) * down, :] = rows_ref[i, part : part + down, :]


def turn_weights(w_at, parts, attn_rows, feed_rows):
    m = len(parts)
    width = parts[0].shape[1]
    rows = width // m + feed_rows // (2 * m)
    return pl.pallas_call(
        turn_weights_kernel,
        out_shape=[
            jax.ShapeDtypeStruct((attn_rows, width), BF),
            jax.ShapeDtypeStruct((feed_rows, width), BF),
        ],
        grid_spec=pltpu.PrefetchScalarGridSpec(
            num_scalar_prefetch=1,
            grid=(1,),
            in_specs=[whole(x.shape) for x in parts],
            out_specs=[whole((attn_rows, width)), whole((feed_rows, width))],
            scratch_shapes=[pltpu.VMEM((m, rows, width), BF)],
        ),
        compiler_params=pltpu.CompilerParams(vmem_limit_bytes=24 << 20),
        cost_estimate=pl.CostEstimate(
            flops=0, bytes_accessed=4 * m * rows * width, transcendentals=0
        ),
        name="turn_weights",
    )(w_at, *parts)


def turn_feed_kernel(part_ref, out_ref):
    m, _, cols = out_ref.shape
    two, width = part_ref.shape
    rows, down = width // m, two // (2 * m)
    up = part_ref[: two // 2, :].astype(F32).T.astype(BF)
    for i in range(m):
        out_ref[i, :rows, :] = up[i * rows : (i + 1) * rows]
        low = part_ref[two // 2 + i * down : two // 2 + (i + 1) * down, :]
        for c in range(width // cols):
            out_ref[i, rows + c * down : rows + (c + 1) * down, :] = low[:, c * cols : (c + 1) * cols]


def turn_attn_kernel(part_ref, out_ref):
    m, rows, _ = out_ref.shape
    turned = part_ref[...].astype(F32).T.astype(BF)
    for i in range(m):
        out_ref[i] = turned[i * rows : (i + 1) * rows]


def turn(kernel, x, *shapes):
    out = [jax.ShapeDtypeStruct(shape, BF) for shape in shapes]
    return pl.pallas_call(
        kernel,
        out_shape=out if len(out) > 1 else out[0],
        compiler_params=pltpu.CompilerParams(vmem_limit_bytes=24 << 20),
        cost_estimate=pl.CostEstimate(flops=0, bytes_accessed=4 * x.size, transcendentals=0),
        name="turn",
    )(x)


def mlp_kernel(group_ids, state_ref, proj_ref, bproj_ref, gain_ref, shift_ref, w_ref, bup_ref, bdown_ref, *refs):
    att_refs, (after_ref, normed_ref, out_ref) = split_refs(refs, GROUPS, 3)
    c = pl.program_id(0)

    @pl.when(c == 0)
    def _():
        after = state_ref[...] + bproj_ref[...]
        for k in range(GROUPS):
            after = after + dot_nn(att_refs[k][...], proj_ref[group_ids[k]])
        after_ref[...] = after
        unit, _ = norm_parts(after)
        normed_ref[...] = (unit * gain_ref[...] + shift_ref[...]).astype(BF)
        out_ref[...] = after + bdown_ref[...]

    part = w_ref.shape[1] // 2
    hidden = gelu_tanh(dot_nt(normed_ref[...], w_ref[0, :part, :]) + bup_ref[0])
    out_ref[...] += dot_nn(hidden.astype(BF), w_ref[0, part:, :])


def mlp(group_ids, state, proj, bproj, gain, shift, w, bup, bdown, atts):
    rows, width = state.shape
    n, two, _ = w.shape
    wide = jax.ShapeDtypeStruct((rows, width), F32)
    return pl.pallas_call(
        mlp_kernel,
        out_shape=[wide, jax.ShapeDtypeStruct((rows, width), BF), wide],
        grid_spec=pltpu.PrefetchScalarGridSpec(
            num_scalar_prefetch=1,
            grid=(n,),
            in_specs=[whole(x.shape) for x in (state, proj, bproj, gain, shift)]
            + [
                pl.BlockSpec((1, two, width), lambda c, *_: (c, 0, 0)),
                pl.BlockSpec((1, 1, two // 2), lambda c, *_: (c, 0, 0)),
                whole(bdown.shape),
            ]
            + [whole(x.shape) for x in atts],
            out_specs=[whole((rows, width))] * 3,
        ),
        compiler_params=pltpu.CompilerParams(vmem_limit_bytes=40 << 20),
        cost_estimate=pl.CostEstimate(
            flops=6 * rows * (w.size + proj.size), bytes_accessed=2 * w.size, transcendentals=0
        ),
        name="mlp",
    )(group_ids, state, proj, bproj, gain, shift, w, bup, bdown, *atts)


def mlp_back_kernel(
    group_ids, grad_ref, after_ref, normed_ref, gain_ref, proj_ref, w_ref, bup_ref, *refs
):
    att_refs, datt_refs, outs, (dx_ref,) = split_refs(refs, GROUPS, GROUPS, 8, 1)
    dw_ref, dproj_ref, gafter_ref, dgain_ref, dshift_ref, dbup_ref, dbdown_ref, dbproj_ref = outs
    c = pl.program_id(0)
    rows, width = grad_ref.shape
    part = w_ref.shape[1] // 2
    grad = grad_ref[...].astype(BF)
    normed = normed_ref[...]
    up, down = w_ref[0, :part, :], w_ref[0, part:, :]
    bias = jnp.broadcast_to(bup_ref[0], (8, part)).T[:, :1]

    @pl.when(c == 0)
    def _():
        dx_ref[...] = jnp.zeros_like(dx_ref)
        dbdown_ref[...] = jnp.sum(grad.astype(F32), axis=0, keepdims=True)

    hid = dot_nt(up, normed) + bias
    square = hid * hid
    th = jnp.tanh(gelu_coeff * (hid + 0.044715 * hid * square))
    value = (0.5 * hid * (1.0 + th)).astype(BF)
    slope = 0.5 * (1.0 + th) + 0.5 * hid * (1.0 - th * th) * gelu_coeff * (
        1.0 + 3 * 0.044715 * square
    )
    ghid = (dot_nt(down, grad) * slope).astype(BF)
    dbup_ref[0] = dot_nt(jnp.ones((8, rows), BF), ghid)
    dw_ref[0, :part, :] = dot_nn(ghid, normed).astype(BF)
    dw_ref[0, part:, :] = dot_nn(value, grad).astype(BF)
    dx_ref[...] += dot_tn(ghid, up)

    @pl.when(c == pl.num_programs(0) - 1)
    def _():
        unit, scale = norm_parts(after_ref[...])
        back, dgain, dshift = norm_back(dx_ref[...], unit, scale, gain_ref[...])
        gafter = grad_ref[...] + back
        gafter_ref[...] = gafter
        dgain_ref[...] = dgain
        dshift_ref[...] = dshift
        gatt = gafter.astype(BF)
        dbproj_ref[...] = jnp.sum(gatt.astype(F32), axis=0, keepdims=True)
        for k in range(GROUPS):
            g = group_ids[k]
            datt_refs[k][...] = dot_nt(gatt, proj_ref[g]).astype(BF)
            dproj_ref[g] = dot_tn(att_refs[k][...], gatt).astype(BF)


def mlp_back(group_ids, grad, after, normed, gain, proj, w, bup, atts):
    rows, width = grad.shape
    n, two, _ = w.shape
    gw = width // GROUPS
    vec = jax.ShapeDtypeStruct((1, width), F32)
    step_w = pl.BlockSpec((1, two, width), lambda c, *_: (c, 0, 0))
    return pl.pallas_call(
        mlp_back_kernel,
        out_shape=[jax.ShapeDtypeStruct((rows, gw), BF)] * GROUPS
        + [
            jax.ShapeDtypeStruct(w.shape, BF),
            jax.ShapeDtypeStruct(proj.shape, BF),
            jax.ShapeDtypeStruct((rows, width), F32),
            vec,
            vec,
            jax.ShapeDtypeStruct((n, 8, two // 2), F32),
            vec,
            vec,
        ],
        grid_spec=pltpu.PrefetchScalarGridSpec(
            num_scalar_prefetch=1,
            grid=(n,),
            in_specs=[whole(x.shape) for x in (grad, after, normed, gain, proj)]
            + [step_w, pl.BlockSpec((1, 1, two // 2), lambda c, *_: (c, 0, 0))]
            + [whole(x.shape) for x in atts],
            out_specs=[whole((rows, gw))] * GROUPS
            + [
                step_w,
                whole(proj.shape),
                whole((rows, width)),
                whole((1, width)),
                whole((1, width)),
                pl.BlockSpec((1, 8, two // 2), lambda c, *_: (c, 0, 0)),
                whole((1, width)),
                whole((1, width)),
            ],
            scratch_shapes=[pltpu.VMEM((rows, width), F32)],
        ),
        compiler_params=pltpu.CompilerParams(vmem_limit_bytes=48 << 20),
        cost_estimate=pl.CostEstimate(
            flops=15 * rows * w.size + 12 * rows * proj.size, bytes_accessed=4 * w.size, transcendentals=0
        ),
        name="mlp_back",
    )(group_ids, grad, after, normed, gain, proj, w, bup, *atts)


def head_masks(rows, width):
    lane = lax.broadcasted_iota(jnp.int32, (rows, width), 1)
    return [
        (lane >= h * HEAD_DIM) & (lane < (h + 1) * HEAD_DIM) for h in range(width // HEAD_DIM)
    ]


def only_head(block, masks):
    wide = block.astype(F32)
    return [jnp.where(mask, wide, 0.0).astype(BF) for mask in masks]


def causal_tile(blk):
    key_at = lax.broadcasted_iota(jnp.int32, (blk, blk), 0)
    query_at = lax.broadcasted_iota(jnp.int32, (blk, blk), 1)
    return key_at <= query_at


def query_part(ref, rows, width):
    low = width // 128 * 128
    high = -(-2 * width // 128) * 128
    window = ref[rows, low:high].astype(F32)
    if width > low:
        window = pltpu.roll(window, high - width, 1)
    return (window[:, :width] * (HEAD_DIM ** (-0.5))).astype(BF)


def attend_kernel(q_id, k_loc, *refs):
    mixed_refs, o_refs, (lse_ref, q_ref, k_ref, vt_ref, acc_ref) = split_refs(
        refs, len(refs) - GROUPS - 5, GROUPS, 5
    )
    q_blocks, blk, width = q_ref.shape
    heads = width // HEAD_DIM

    for r, ref in enumerate(mixed_refs):
        for b in range(2):
            rows = slice(b * blk, (b + 1) * blk)
            k_ref[2 * r + b] = ref[rows, :width]
            vt_ref[2 * r + b] = ref[rows, 2 * width :].astype(F32).T.astype(BF)
            if r < GROUPS:
                q_ref[2 * r + b] = query_part(ref, rows, width)
    masks = head_masks(blk, width)

    def per_query(qb):
        q_blk = q_ref[qb]
        q_h = only_head(q_blk, masks)
        own = q_id[qb]
        loc = k_loc[own]
        keys = k_ref[loc]
        tri = causal_tile(blk)
        stats = []
        for h in range(heads):
            rows = slice(h * HEAD_DIM, (h + 1) * HEAD_DIM)
            s = jnp.where(tri, dot_nt(keys, q_h[h]), -1e30)
            top = jnp.max(s, axis=0, keepdims=True)
            p = jnp.exp(s - top)
            stats.append((top, jnp.sum(p, axis=0, keepdims=True)))
            acc_ref[rows, :] = dot_nn(vt_ref[loc, rows, :], p.astype(BF))

        def step(i, carry):
            loc = k_loc[i]
            keys = k_ref[loc]
            out = []
            for h in range(heads):
                rows = slice(h * HEAD_DIM, (h + 1) * HEAD_DIM)
                top, total = carry[h]
                s = dot_nt(keys, q_h[h])
                new = jnp.maximum(top, jnp.max(s, axis=0, keepdims=True))
                alpha = jnp.exp(top - new)
                p = jnp.exp(s - new)
                out.append((new, total * alpha + jnp.sum(p, axis=0, keepdims=True)))
                acc_ref[rows, :] = acc_ref[rows, :] * alpha + dot_nn(
                    vt_ref[loc, rows, :], p.astype(BF)
                )
            return tuple(out)

        stats = lax.fori_loop(0, own, step, tuple(stats))
        for h in range(heads):
            rows = slice(h * HEAD_DIM, (h + 1) * HEAD_DIM)
            top, total = stats[h]
            acc_ref[rows, :] = acc_ref[rows, :] / total
            lse_ref[qb, h : h + 1, :] = top + jnp.log(total)
        return acc_ref[...].T.astype(BF)

    for k in range(GROUPS):

        def pair(b, _, k=k):
            start = pl.multiple_of(b * blk, 32)
            o_refs[k][pl.ds(start, blk), :] = per_query(2 * k + b)
            return 0

        lax.fori_loop(0, 2, pair, 0)


def attend(q_id, k_loc, mixed):
    rows, cols = mixed[0].shape
    blk, width = rows // 2, cols // 3
    q_blocks, k_blocks = 2 * GROUPS, 2 * len(mixed)
    return pl.pallas_call(
        attend_kernel,
        out_shape=[jax.ShapeDtypeStruct((rows, width), BF)] * GROUPS
        + [jax.ShapeDtypeStruct((q_blocks, 8, blk), F32)],
        grid_spec=pltpu.PrefetchScalarGridSpec(
            num_scalar_prefetch=2,
            grid=(1,),
            in_specs=[whole(x.shape) for x in mixed],
            out_specs=[whole((rows, width))] * GROUPS + [whole((q_blocks, 8, blk))],
            scratch_shapes=[
                pltpu.VMEM((q_blocks, blk, width), BF),
                pltpu.VMEM((k_blocks, blk, width), BF),
                pltpu.VMEM((k_blocks, width, blk), BF),
                pltpu.VMEM((width, blk), F32),
            ],
        ),
        compiler_params=pltpu.CompilerParams(vmem_limit_bytes=48 << 20),
        cost_estimate=pl.CostEstimate(
            flops=40 * q_blocks * k_blocks * blk * blk * width,
            bytes_accessed=2 * len(mixed) * rows * cols,
            transcendentals=q_blocks * k_blocks * blk * blk * 2,
        ),
        name="attend",
    )(q_id, k_loc, *mixed)


def attend_back_kernel(q_id, k_loc, *refs):
    count = (len(refs) - 2 * GROUPS - 9) // 2
    mixed_refs, o_refs, do_refs, (lse_ref,), dm_refs, scratch = split_refs(
        refs, count, GROUPS, GROUPS, 1, count, 8
    )
    q_ref, k_ref, v_ref, kt_ref, dq_ref, dka_ref, dva_ref, dqt_ref = scratch
    q_blocks, blk, width = q_ref.shape
    heads = width // HEAD_DIM
    for r, ref in enumerate(mixed_refs):
        for b in range(2):
            rows = slice(b * blk, (b + 1) * blk)
            at = 2 * r + b
            keys = ref[rows, :width]
            k_ref[at] = keys
            kt_ref[at] = keys.astype(F32).T.astype(BF)
            v_ref[at] = ref[rows, 2 * width :]
            if r < GROUPS:
                q_ref[at] = query_part(ref, rows, width)

    def clear(b, _):
        dka_ref[b] = jnp.zeros((blk, width), F32)
        dva_ref[b] = jnp.zeros((blk, width), F32)
        return 0

    lax.fori_loop(0, k_ref.shape[0], clear, 0)
    masks = head_masks(blk, width)

    def per_query(qb, do_blk, o_blk):
        q_blk = q_ref[qb]
        q_h = only_head(q_blk, masks)
        do_h = only_head(do_blk, masks)
        both = (do_blk.astype(F32) * o_blk.astype(F32)).T
        delta = [
            jnp.sum(both[h * HEAD_DIM : (h + 1) * HEAD_DIM], axis=0, keepdims=True)
            for h in range(heads)
        ]
        lse = [lse_ref[qb, h : h + 1, :] for h in range(heads)]
        own = q_id[qb]

        def tile(loc, tri, first):
            keys = k_ref[loc]
            values = v_ref[loc]
            dk = dka_ref[loc]
            dv = dva_ref[loc]
            for h in range(heads):
                rows = slice(h * HEAD_DIM, (h + 1) * HEAD_DIM)
                p = jnp.exp(dot_nt(keys, q_h[h]) - lse[h])
                if tri is not None:
                    p = jnp.where(tri, p, 0.0)
                dp = dot_nt(values, do_h[h])
                ds = (p * (dp - delta[h])).astype(BF)
                dv = dv + dot_nn(p.astype(BF), do_h[h])
                dk = dk + dot_nn(ds, q_h[h])
                dq = dot_nn(kt_ref[loc, rows, :], ds)
                dqt_ref[rows, :] = dq if first else dqt_ref[rows, :] + dq
            dka_ref[loc] = dk
            dva_ref[loc] = dv

        tile(k_loc[own], causal_tile(blk), True)

        def step(i, _):
            tile(k_loc[i], None, False)
            return 0

        lax.fori_loop(0, own, step, 0)
        dq_ref[qb] = (dqt_ref[...] * (HEAD_DIM ** (-0.5))).T

    for k in range(GROUPS):

        def pair(b, _, k=k):
            rows = pl.ds(pl.multiple_of(b * blk, 32), blk)
            per_query(2 * k + b, do_refs[k][rows, :], o_refs[k][rows, :])
            return 0

        lax.fori_loop(0, 2, pair, 0)

    for r, ref in enumerate(dm_refs):

        def finish(b, _, r=r, ref=ref):
            at = 2 * r + b
            dq = dq_ref[at] if r < GROUPS else jnp.zeros((blk, width), F32)
            joined = jnp.concatenate([dka_ref[at], dq, dva_ref[at]], 1)
            ref[pl.ds(pl.multiple_of(b * blk, 32), blk), :] = joined.astype(BF)
            return 0

        lax.fori_loop(0, 2, finish, 0)


def attend_back(q_id, k_loc, mixed, o, do, lse):
    rows, cols = mixed[0].shape
    blk, width = rows // 2, cols // 3
    q_blocks, k_blocks = 2 * GROUPS, 2 * len(mixed)
    return pl.pallas_call(
        attend_back_kernel,
        out_shape=[jax.ShapeDtypeStruct((rows, cols), BF)] * len(mixed),
        grid_spec=pltpu.PrefetchScalarGridSpec(
            num_scalar_prefetch=2,
            grid=(1,),
            in_specs=[whole(x.shape) for x in (*mixed, *o, *do, lse)],
            out_specs=[whole((rows, cols))] * len(mixed),
            scratch_shapes=[
                pltpu.VMEM((q_blocks, blk, width), BF),
                pltpu.VMEM((k_blocks, blk, width), BF),
                pltpu.VMEM((k_blocks, blk, width), BF),
                pltpu.VMEM((k_blocks, width, blk), BF),
                pltpu.VMEM((q_blocks, blk, width), F32),
                pltpu.VMEM((k_blocks, blk, width), F32),
                pltpu.VMEM((k_blocks, blk, width), F32),
                pltpu.VMEM((width, blk), F32),
            ],
        ),
        compiler_params=pltpu.CompilerParams(vmem_limit_bytes=56 << 20),
        cost_estimate=pl.CostEstimate(
            flops=70 * q_blocks * k_blocks * blk * blk * width,
            bytes_accessed=4 * len(mixed) * rows * cols,
            transcendentals=q_blocks * k_blocks * blk * blk * 2,
        ),
        name="attend_back",
    )(q_id, k_loc, *mixed, *o, *do, lse)


def swap(x, axis_name, size, k):
    return lax.ppermute(x, axis_name, [(i, i ^ k) for i in range(size)])


def pick(x, at):
    return lax.dynamic_index_in_dim(x, at, 0, keepdims=False)


class Place:
    def __init__(self, n, m):
        self.n, self.m = n, m
        self.inner = n // GROUPS
        self.idx = lax.axis_index("ctx")
        self.outer_at = self.idx // self.inner
        self.inner_at = self.idx % self.inner
        self.w = lax.axis_index("wt")

    def exchange(self, parts):
        return [parts[0]] + [
            swap(parts[k], "ctx", self.n, k * self.inner) for k in range(1, GROUPS)
        ]

    def scatter_ctx(self, x):
        return lax.psum_scatter(x, "ctx", scatter_dimension=0, tiled=True)

    def gather_ctx(self, x):
        return lax.all_gather(x, "ctx", axis=0, tiled=False)

    def scatter_wt(self, x):
        total = pick(x, self.w).astype(F32)
        for k in range(1, self.m):
            total = total + swap(pick(x, self.w ^ k), "wt", self.m, k).astype(F32)
        return total

    def total(self, x):
        for axis_name, size in (("ctx", self.n), ("wt", self.m)):
            k = 1
            while k < size:
                x = x + swap(x, axis_name, size, k)
                k *= 2
        return x


def split_columns(shard, at, count, groups):
    rows, cols = shard.shape
    c = cols // (groups * count)
    cut = shard.reshape(rows, groups, count, c)
    return lax.dynamic_index_in_dim(cut, at, 2, keepdims=False).reshape(rows, groups * c)


def qkv_piece(shard, place):
    rows, cols = shard.shape
    cut = shard.reshape(rows, 3, GROUPS, cols // (3 * GROUPS))
    own = lax.dynamic_index_in_dim(cut, place.outer_at, 2, keepdims=False)
    own = jnp.concatenate([own[:, 1], own[:, 0], own[:, 2]], 1)
    part = own.shape[1] // place.inner
    return lax.dynamic_slice_in_dim(own, place.inner_at * part, part, 1)


def after(x, done):
    return lax.optimization_barrier((x, done))[0]


def pack_layer(place, matrices, layer):
    qkv_weight, out_weight, up_weight, down_weight = matrices
    n, m = place.n, place.m
    width, ff = out_weight.shape[2], up_weight.shape[2]
    columns = jnp.concatenate(
        [
            qkv_piece(qkv_weight[layer], place),
            split_columns(out_weight[layer], place.idx, n, 1),
            split_columns(up_weight[layer], place.idx, n, m),
        ],
        1,
    )
    pad = -columns.shape[1] % width
    assert pad == 0 or columns.shape[1] < width
    if pad:
        columns = jnp.pad(columns, ((0, 0), (0, pad)))
    down = pick(down_weight[layer].reshape(n, ff // (n * m), width), place.idx)
    return jnp.concatenate([columns, down], 0)


def pack_small(small, width):
    flat = [s.reshape(-1) for s in small]
    size = sum(f.shape[0] for f in flat)
    extra = -(-size // (width * 16)) * 16
    flat.append(jnp.zeros((extra * width - size,), BF))
    return jnp.concatenate(flat).reshape(extra, width)


def unpack_small(place, parts, small):
    got = jnp.stack([pick(jnp.stack(parts), place.w ^ i) for i in range(place.m)])
    got = got.reshape(place.m, -1)
    out, at = [], 0
    for s in small:
        count, c = s.shape
        part = got[:, at : at + count * c].reshape(place.m, count, c)
        out.append(part.transpose(1, 0, 2).reshape(count, place.m * c).astype(F32))
        at += count * c
    return out


def spread_wt(place, x):
    return [x] + [swap(x, "wt", place.m, k) for k in range(1, place.m)]


def scatter_part(place, dw):
    return place.scatter_ctx(dw.reshape(-1, dw.shape[2]))


def own_part(place, part, kernel, rows):
    turned = turn(kernel, part, (place.m, rows, part.size // (place.m * rows)))
    return place.scatter_wt(turned).astype(BF)


def unpack_feed(place, own, ff, width):
    n, m = place.n, place.m
    rows = width // m
    up, down = own[:, :rows], own[:, rows:]
    up = up.reshape(n, rows, m, ff // (n * m)).transpose(1, 2, 0, 3).reshape(rows, ff)
    down = down.reshape(n, -1, ff // (n * m), down.shape[2]).transpose(0, 2, 1, 3)
    return up.astype(F32), down.reshape(ff // m, width).astype(F32)


def unpack_attn(place, own, width):
    n, m = place.n, place.m
    rows = 3 * width // n
    gw = width // GROUPS
    qkv, proj = own[:, :, :rows], own[:, :, rows:]
    qkv = qkv.reshape(GROUPS, place.inner, width // m, rows).transpose(2, 0, 1, 3)
    qkv = qkv.reshape(width // m, GROUPS, 3, gw)
    qkv = jnp.concatenate([qkv[:, :, i].reshape(width // m, width) for i in (1, 0, 2)], 1)
    proj = proj.transpose(1, 0, 2).reshape(width // m, width)
    return qkv.astype(F32), proj.astype(F32)


def reduce_small(place, smalls):
    sizes = [v.shape[0] for v in smalls[0]]
    packed = jnp.concatenate([v for layer in smalls for v in layer]).reshape(-1, 128)
    packed = place.total(packed).reshape(len(smalls), -1)
    out, at = [], 0
    for size in sizes:
        part = packed[:, at : at + size].reshape(len(smalls), place.m, size // place.m)
        out.append(lax.dynamic_index_in_dim(part, place.w, 1, keepdims=False))
        at += size
    return out


def body(
    n, m, inputs, block_table, ln1_gain, ln1_bias, qkv_weight, query_bias, value_bias, out_weight,
    out_bias, ln2_gain, ln2_bias, up_weight, up_bias, down_weight, down_bias, cotangent,
):
    place = Place(n, m)
    rows, width = inputs.shape[1:]
    ff = up_weight.shape[2]
    gw = width // GROUPS
    group_ids = jnp.stack([place.outer_at ^ k for k in range(GROUPS)]).astype(jnp.int32)
    key_ids = jnp.concatenate(
        [
            pick(block_table, place.idx ^ (k * place.inner + j))
            for j in range(place.inner)
            for k in range(GROUPS)
        ]
    ).astype(jnp.int32)
    q_id = key_ids[: 2 * GROUPS]
    at = jnp.arange(2 * n, dtype=jnp.int32)
    k_loc = jnp.sum(jnp.where(key_ids[None, :] == at[:, None], at[None, :], 0), axis=1).astype(jnp.int32)

    small = (ln1_gain, ln1_bias, query_bias, value_bias, out_bias, ln2_gain, ln2_bias, up_bias, down_bias)
    matrices = (qkv_weight, out_weight, up_weight, down_weight)
    w_at = place.w.astype(jnp.int32).reshape(1)
    attn_rows, feed_rows = 4 * width // n, 2 * ff // n
    big_rows = width // m + ff // (n * m)
    first = jnp.concatenate([pack_layer(place, matrices, 0), pack_small(small, width)], 0)
    parts = spread_wt(place, first)
    vectors = unpack_small(place, [p[big_rows:] for p in parts], small)
    attn, feed = turn_weights(w_at, parts, attn_rows, feed_rows)
    attn = place.gather_ctx(attn)
    weights = [(attn, place.gather_ctx(after(feed, attn)))]
    params = []
    for layer in range(LAYERS):
        v = [x[layer].reshape(1, -1) for x in vectors]
        bias = jnp.concatenate(
            [jnp.zeros((GROUPS, 1, gw), F32), v[2].reshape(GROUPS, 1, gw), v[3].reshape(GROUPS, 1, gw)], 2
        )
        bup = v[7].reshape(m, n, ff // (n * m)).transpose(1, 0, 2).reshape(n, 1, ff // n)
        params.append((v, bias, bup))

    state = inputs[0].astype(F32)
    saved = []
    for layer in range(LAYERS):
        attn, feed = weights[layer]
        v, bias, bup = params[layer]
        *mixed, normed, proj = mix(group_ids, state, v[0], v[1], attn, bias)
        mixed = place.exchange(mixed)
        if layer + 1 < LAYERS:
            send = after(pack_layer(place, matrices, layer + 1), parts[1])
            parts = spread_wt(place, send)
        mixed = mixed + [
            swap(x, "ctx", n, j) for j in range(1, place.inner) for x in mixed
        ]
        *o, lse = attend(q_id, k_loc, mixed)
        if layer + 1 < LAYERS:
            next_attn, next_feed = turn_weights(w_at, parts, attn_rows, feed_rows)
            next_attn = place.gather_ctx(after(next_attn, (feed, mixed)))
            weights.append((next_attn, place.gather_ctx(after(next_feed, (next_attn, o[0])))))
        atts = place.exchange(o)
        mid, normed_two, new = mlp(
            group_ids, state, proj, v[4], v[5], v[6], feed, bup, v[8], atts
        )
        saved.append((state, normed, mixed, o, lse, atts, mid, normed_two, proj))
        state = new
    outputs = state.astype(BF)[None]
    gradient = cotangent[0].astype(F32)
    shards, smalls, pending = [None] * LAYERS, [None] * LAYERS, []
    for layer in reversed(range(LAYERS)):
        attn, feed = weights[layer]
        v, bias, bup = params[layer]
        before, normed, mixed, o, lse, atts, mid, normed_two, proj = saved[layer]
        *datts, dfeed, dproj, gafter, dgain2, dshift2, dbup, dbdown, dbproj = mlp_back(
            group_ids, gradient, mid, normed_two, v[5], proj, feed, bup, atts
        )
        part_feed = scatter_part(place, dfeed)
        do = place.exchange(datts)
        dm = attend_back(q_id, k_loc, mixed, o, do, lse)
        dm = list(dm)
        if layer > 0:
            dm[0] = after(dm[0], part_feed)
        if layer + 1 < LAYERS:
            part_attn = after(part_attn, dm[1])
            pending.append(own_part(place, part_attn, turn_attn_kernel, width // m))
        part_feed = after(part_feed, dm[1])
        pending.append(own_part(place, part_feed, turn_feed_kernel, 2 * width // m))
        own = []
        for k in range(GROUPS):
            if place.inner == 1:
                own.append(dm[k])
                continue
            total = dm[k].astype(F32)
            for j in range(1, place.inner):
                total = total + swap(dm[j * GROUPS + k], "ctx", n, j).astype(F32)
            own.append(total.astype(BF))
        gms = place.exchange(own)
        dmix, gradient, dgain1, dshift1, dbias = mix_back(
            group_ids, gafter, before, v[0], normed, attn, dproj, gms
        )
        if layer == 0:
            joined = place.gather_ctx(jnp.concatenate(pending, 0))
            dmix = after(dmix, joined)
        part_attn = scatter_part(place, dmix)
        dbup = dbup[:, 0].reshape(n, m, ff // (n * m)).transpose(1, 0, 2)
        smalls[layer] = [
            x.reshape(-1)
            for x in (
                dgain1, dshift1, dbias[:, 0, gw : 2 * gw], dbias[:, 0, 2 * gw :], dbproj,
                dgain2, dshift2, dbup, dbdown,
            )
        ]
    own_attn = place.gather_ctx(own_part(place, part_attn, turn_attn_kernel, width // m))
    counts, at, owns = [p.shape[0] for p in pending], 0, []
    for count in counts:
        owns.append(joined[:, at : at + count])
        at += count
    for layer in range(LAYERS):
        own_feed = owns[2 * (LAYERS - 1 - layer)]
        part = own_attn if layer == 0 else owns[2 * (LAYERS - 1 - layer) + 1]
        shards[layer] = unpack_attn(place, part, width) + unpack_feed(place, own_feed, ff, width)
    vec = reduce_small(place, smalls)
    mixw, projw, up, down = [jnp.stack([s[i] for s in shards]) for i in range(4)]
    return (
        outputs, gradient[None], vec[0], vec[1], mixw, vec[2], vec[3], projw, vec[4],
        vec[5], vec[6], up, vec[7], down, vec[8],
    )


def solution(mesh):
    row, vec, mat = P("wt", "ctx", None), P(None, "wt"), P(None, "wt", None)
    in_specs = (row, P(), vec, vec, mat, vec, vec, mat, vec, vec, vec, mat, vec, mat, vec, row)
    out_specs = (row, row, vec, vec, mat, vec, vec, mat, vec, vec, vec, mat, vec, mat, vec)
    return jax.shard_map(
        functools.partial(body, mesh.shape["ctx"], mesh.shape["wt"]),
        mesh=mesh,
        in_specs=in_specs,
        out_specs=out_specs,
        check_vma=False,
    )
```

```python
import functools

import jax
import jax.numpy as jnp
from jax import lax
from jax.experimental import pallas as pl
from jax.experimental.pallas import tpu as pltpu
from jax.sharding import PartitionSpec as P

HEAD_DIM = 64
LAYERS = 2
GROUPS = 4

epsilon = 1e-05
gelu_coeff = 0.7978845608028654
BF = jnp.bfloat16
F32 = jnp.float32


def gelu_tanh(values):
    return (
        0.5 * values * (1.0 + jnp.tanh(gelu_coeff * (values + 0.044715 * values * values * values)))
    )


def dot_nt(a, b):
    return lax.dot_general(a, b, (((1,), (1,)), ((), ())), preferred_element_type=F32)


def dot_nn(a, b):
    return lax.dot_general(a, b, (((1,), (0,)), ((), ())), preferred_element_type=F32)


def dot_tn(a, b):
    return lax.dot_general(a, b, (((0,), (0,)), ((), ())), preferred_element_type=F32)


def whole(shape):
    return pl.BlockSpec(shape, lambda *_: (0,) * len(shape))


def norm_parts(values):
    mean = jnp.mean(values, axis=-1, keepdims=True)
    centred = values - mean
    var = jnp.mean(centred * centred, axis=-1, keepdims=True)
    scale = lax.rsqrt(var + epsilon)
    return centred * scale, scale


def norm_back(grad, unit, scale, gain):
    inner = grad * gain
    a = jnp.mean(inner, axis=-1, keepdims=True)
    b = jnp.mean(inner * unit, axis=-1, keepdims=True)
    return (
        scale * (inner - a - unit * b),
        jnp.sum(grad * unit, axis=0, keepdims=True),
        jnp.sum(grad, axis=0, keepdims=True),
    )


def split_refs(refs, *counts):
    out, at = [], 0
    for count in counts:
        out.append(refs[at : at + count])
        at += count
    return out


def mix_kernel(qkv_rows, group_ids, state_ref, gain_ref, shift_ref, w_ref, bias_ref, *refs):
    out_refs, (normed_ref, proj_ref) = split_refs(refs, GROUPS, 2)
    inner = w_ref.shape[0] // GROUPS
    unit, _ = norm_parts(state_ref[...])
    normed = (unit * gain_ref[...] + shift_ref[...]).astype(BF)
    normed_ref[...] = normed
    for k in range(GROUPS):
        g = group_ids[k]
        w = jnp.concatenate([w_ref[g * inner + e, :qkv_rows, :] for e in range(inner)], 0)
        out_refs[k][...] = (dot_nt(normed, w) + bias_ref[g]).astype(BF)
    proj = jnp.concatenate([w_ref[c, qkv_rows:, :] for c in range(w_ref.shape[0])], 0)
    proj = proj.astype(F32).T.astype(BF)
    gw = proj_ref.shape[1]
    for g in range(GROUPS):
        proj_ref[g] = proj[g * gw : (g + 1) * gw]


def mix(group_ids, state, gain, shift, w, bias):
    rows, width = state.shape
    cols = bias.shape[2]
    inner = w.shape[0] // GROUPS
    return pl.pallas_call(
        functools.partial(mix_kernel, cols // inner),
        out_shape=[jax.ShapeDtypeStruct((rows, cols), BF)] * GROUPS
        + [
            jax.ShapeDtypeStruct((rows, width), BF),
            jax.ShapeDtypeStruct((GROUPS, width // GROUPS, width), BF),
        ],
        grid_spec=pltpu.PrefetchScalarGridSpec(
            num_scalar_prefetch=1,
            grid=(1,),
            in_specs=[whole(state.shape), whole(gain.shape), whole(shift.shape), whole(w.shape), whole(bias.shape)],
            out_specs=[whole((rows, cols))] * GROUPS
            + [whole((rows, width)), whole((GROUPS, width // GROUPS, width))],
        ),
        compiler_params=pltpu.CompilerParams(vmem_limit_bytes=40 << 20),
        cost_estimate=pl.CostEstimate(
            flops=2 * rows * width * cols * GROUPS, bytes_accessed=2 * w.size, transcendentals=0
        ),
        name="mix",
    )(group_ids, state, gain, shift, w, bias)


def mix_back_kernel(
    qkv_rows, group_ids, grad_ref, state_ref, gain_ref, normed_ref, w_ref, dproj_ref, *refs
):
    gm_refs, (dw_ref, out_ref, dgain_ref, dshift_ref, dbias_ref) = split_refs(refs, GROUPS, 5)
    inner = w_ref.shape[0] // GROUPS
    rows = state_ref.shape[0]
    normed = normed_ref[...]
    ones = jnp.ones((8, rows), BF)
    total = None
    for k in range(GROUPS):
        g = group_ids[k]
        gm = gm_refs[k][...]
        w = jnp.concatenate([w_ref[g * inner + e, :qkv_rows, :] for e in range(inner)], 0)
        part = dot_nn(gm, w)
        total = part if total is None else total + part
        dw = dot_tn(gm, normed).astype(BF)
        for e in range(inner):
            dw_ref[g * inner + e, :qkv_rows, :] = dw[e * qkv_rows : (e + 1) * qkv_rows]
        dbias_ref[g] = dot_nn(ones, gm)
    dproj = jnp.concatenate([dproj_ref[g] for g in range(GROUPS)], 0)
    dproj = dproj.astype(F32).T.astype(BF)
    part = dproj.shape[0] // dw_ref.shape[0]
    for c in range(dw_ref.shape[0]):
        dw_ref[c, qkv_rows:, :] = dproj[c * part : (c + 1) * part]
    unit, scale = norm_parts(state_ref[...])
    back, dgain, dshift = norm_back(total, unit, scale, gain_ref[...])
    out_ref[...] = grad_ref[...] + back
    dgain_ref[...] = dgain
    dshift_ref[...] = dshift


def mix_back(group_ids, grad_after, state, gain, normed, w, dproj, gms):
    rows, width = state.shape
    cols = gms[0].shape[1]
    n = w.shape[0]
    inner = n // GROUPS
    vec = jax.ShapeDtypeStruct((1, width), F32)
    return pl.pallas_call(
        functools.partial(mix_back_kernel, cols // inner),
        out_shape=[
            jax.ShapeDtypeStruct(w.shape, BF),
            jax.ShapeDtypeStruct((rows, width), F32),
            vec,
            vec,
            jax.ShapeDtypeStruct((GROUPS, 8, cols), F32),
        ],
        grid_spec=pltpu.PrefetchScalarGridSpec(
            num_scalar_prefetch=1,
            grid=(1,),
            in_specs=[whole(x.shape) for x in (grad_after, state, gain, normed, w, dproj, *gms)],
            out_specs=[
                whole(w.shape),
                whole((rows, width)),
                whole((1, width)),
                whole((1, width)),
                whole((GROUPS, 8, cols)),
            ],
        ),
        compiler_params=pltpu.CompilerParams(vmem_limit_bytes=52 << 20),
        cost_estimate=pl.CostEstimate(
            flops=12 * rows * width * cols * GROUPS, bytes_accessed=4 * w.size, transcendentals=0
        ),
        name="mix_back",
    )(group_ids, grad_after, state, gain, normed, w, dproj, *gms)


def turn_weights_kernel(w_at, *refs):
    parts, (attn_ref, feed_ref, rows_ref) = split_refs(refs, len(refs) - 3, 3)
    m = len(parts)
    attn_rows, width = attn_ref.shape
    part = width // m
    up = feed_ref.shape[0] // 2
    down = up // m
    for k, ref in enumerate(parts):
        rows_ref[w_at[0] ^ k] = ref[: part + down, :]
    turned = jnp.concatenate([rows_ref[i, :part, :] for i in range(m)], 0)
    turned = turned.astype(F32).T.astype(BF)
    attn_ref[...] = turned[:attn_rows]
    feed_ref[:up, :] = turned[attn_rows : attn_rows + up]
    for i in range(m):
        feed_ref[up + i * down : up + (i + 1) * down, :] = rows_ref[i, part : part + down, :]


def turn_weights(w_at, parts, attn_rows, feed_rows):
    m = len(parts)
    width = parts[0].shape[1]
    rows = width // m + feed_rows // (2 * m)
    return pl.pallas_call(
        turn_weights_kernel,
        out_shape=[
            jax.ShapeDtypeStruct((attn_rows, width), BF),
            jax.ShapeDtypeStruct((feed_rows, width), BF),
        ],
        grid_spec=pltpu.PrefetchScalarGridSpec(
            num_scalar_prefetch=1,
            grid=(1,),
            in_specs=[whole(x.shape) for x in parts],
            out_specs=[whole((attn_rows, width)), whole((feed_rows, width))],
            scratch_shapes=[pltpu.VMEM((m, rows, width), BF)],
        ),
        compiler_params=pltpu.CompilerParams(vmem_limit_bytes=24 << 20),
        cost_estimate=pl.CostEstimate(
            flops=0, bytes_accessed=4 * m * rows * width, transcendentals=0
        ),
        name="turn_weights",
    )(w_at, *parts)


def turn_feed_kernel(part_ref, out_ref):
    m, _, cols = out_ref.shape
    two, width = part_ref.shape
    rows, down = width // m, two // (2 * m)
    up = part_ref[: two // 2, :].astype(F32).T.astype(BF)
    for i in range(m):
        out_ref[i, :rows, :] = up[i * rows : (i + 1) * rows]
        low = part_ref[two // 2 + i * down : two // 2 + (i + 1) * down, :]
        for c in range(width // cols):
            out_ref[i, rows + c * down : rows + (c + 1) * down, :] = low[:, c * cols : (c + 1) * cols]


def turn_attn_kernel(part_ref, out_ref):
    m, rows, _ = out_ref.shape
    turned = part_ref[...].astype(F32).T.astype(BF)
    for i in range(m):
        out_ref[i] = turned[i * rows : (i + 1) * rows]


def turn(kernel, x, *shapes):
    out = [jax.ShapeDtypeStruct(shape, BF) for shape in shapes]
    return pl.pallas_call(
        kernel,
        out_shape=out if len(out) > 1 else out[0],
        compiler_params=pltpu.CompilerParams(vmem_limit_bytes=24 << 20),
        cost_estimate=pl.CostEstimate(flops=0, bytes_accessed=4 * x.size, transcendentals=0),
        name="turn",
    )(x)


def mlp_kernel(group_ids, state_ref, proj_ref, bproj_ref, gain_ref, shift_ref, w_ref, bup_ref, bdown_ref, *refs):
    att_refs, (after_ref, normed_ref, out_ref) = split_refs(refs, GROUPS, 3)
    c = pl.program_id(0)

    @pl.when(c == 0)
    def _():
        after = state_ref[...] + bproj_ref[...]
        for k in range(GROUPS):
            after = after + dot_nn(att_refs[k][...], proj_ref[group_ids[k]])
        after_ref[...] = after
        unit, _ = norm_parts(after)
        normed_ref[...] = (unit * gain_ref[...] + shift_ref[...]).astype(BF)
        out_ref[...] = after + bdown_ref[...]

    part = w_ref.shape[1] // 2
    hidden = gelu_tanh(dot_nt(normed_ref[...], w_ref[0, :part, :]) + bup_ref[0])
    out_ref[...] += dot_nn(hidden.astype(BF), w_ref[0, part:, :])


def mlp(group_ids, state, proj, bproj, gain, shift, w, bup, bdown, atts):
    rows, width = state.shape
    n, two, _ = w.shape
    wide = jax.ShapeDtypeStruct((rows, width), F32)
    return pl.pallas_call(
        mlp_kernel,
        out_shape=[wide, jax.ShapeDtypeStruct((rows, width), BF), wide],
        grid_spec=pltpu.PrefetchScalarGridSpec(
            num_scalar_prefetch=1,
            grid=(n,),
            in_specs=[whole(x.shape) for x in (state, proj, bproj, gain, shift)]
            + [
                pl.BlockSpec((1, two, width), lambda c, *_: (c, 0, 0)),
                pl.BlockSpec((1, 1, two // 2), lambda c, *_: (c, 0, 0)),
                whole(bdown.shape),
            ]
            + [whole(x.shape) for x in atts],
            out_specs=[whole((rows, width))] * 3,
        ),
        compiler_params=pltpu.CompilerParams(vmem_limit_bytes=40 << 20),
        cost_estimate=pl.CostEstimate(
            flops=6 * rows * (w.size + proj.size), bytes_accessed=2 * w.size, transcendentals=0
        ),
        name="mlp",
    )(group_ids, state, proj, bproj, gain, shift, w, bup, bdown, *atts)


def mlp_back_kernel(
    group_ids, grad_ref, after_ref, normed_ref, gain_ref, proj_ref, w_ref, bup_ref, *refs
):
    att_refs, datt_refs, outs, (dx_ref,) = split_refs(refs, GROUPS, GROUPS, 8, 1)
    dw_ref, dproj_ref, gafter_ref, dgain_ref, dshift_ref, dbup_ref, dbdown_ref, dbproj_ref = outs
    c = pl.program_id(0)
    rows, width = grad_ref.shape
    part = w_ref.shape[1] // 2
    grad = grad_ref[...].astype(BF)
    normed = normed_ref[...]
    up, down = w_ref[0, :part, :], w_ref[0, part:, :]
    bias = jnp.broadcast_to(bup_ref[0], (8, part)).T[:, :1]

    @pl.when(c == 0)
    def _():
        dx_ref[...] = jnp.zeros_like(dx_ref)
        dbdown_ref[...] = jnp.sum(grad.astype(F32), axis=0, keepdims=True)

    hid = dot_nt(up, normed) + bias
    square = hid * hid
    th = jnp.tanh(gelu_coeff * (hid + 0.044715 * hid * square))
    value = (0.5 * hid * (1.0 + th)).astype(BF)
    slope = 0.5 * (1.0 + th) + 0.5 * hid * (1.0 - th * th) * gelu_coeff * (
        1.0 + 3 * 0.044715 * square
    )
    ghid = (dot_nt(down, grad) * slope).astype(BF)
    dbup_ref[0] = dot_nt(jnp.ones((8, rows), BF), ghid)
    dw_ref[0, :part, :] = dot_nn(ghid, normed).astype(BF)
    dw_ref[0, part:, :] = dot_nn(value, grad).astype(BF)
    dx_ref[...] += dot_tn(ghid, up)

    @pl.when(c == pl.num_programs(0) - 1)
    def _():
        unit, scale = norm_parts(after_ref[...])
        back, dgain, dshift = norm_back(dx_ref[...], unit, scale, gain_ref[...])
        gafter = grad_ref[...] + back
        gafter_ref[...] = gafter
        dgain_ref[...] = dgain
        dshift_ref[...] = dshift
        gatt = gafter.astype(BF)
        dbproj_ref[...] = jnp.sum(gatt.astype(F32), axis=0, keepdims=True)
        for k in range(GROUPS):
            g = group_ids[k]
            datt_refs[k][...] = dot_nt(gatt, proj_ref[g]).astype(BF)
            dproj_ref[g] = dot_tn(att_refs[k][...], gatt).astype(BF)


def mlp_back(group_ids, grad, after, normed, gain, proj, w, bup, atts):
    rows, width = grad.shape
    n, two, _ = w.shape
    gw = width // GROUPS
    vec = jax.ShapeDtypeStruct((1, width), F32)
    step_w = pl.BlockSpec((1, two, width), lambda c, *_: (c, 0, 0))
    return pl.pallas_call(
        mlp_back_kernel,
        out_shape=[jax.ShapeDtypeStruct((rows, gw), BF)] * GROUPS
        + [
            jax.ShapeDtypeStruct(w.shape, BF),
            jax.ShapeDtypeStruct(proj.shape, BF),
            jax.ShapeDtypeStruct((rows, width), F32),
            vec,
            vec,
            jax.ShapeDtypeStruct((n, 8, two // 2), F32),
            vec,
            vec,
        ],
        grid_spec=pltpu.PrefetchScalarGridSpec(
            num_scalar_prefetch=1,
            grid=(n,),
            in_specs=[whole(x.shape) for x in (grad, after, normed, gain, proj)]
            + [step_w, pl.BlockSpec((1, 1, two // 2), lambda c, *_: (c, 0, 0))]
            + [whole(x.shape) for x in atts],
            out_specs=[whole((rows, gw))] * GROUPS
            + [
                step_w,
                whole(proj.shape),
                whole((rows, width)),
                whole((1, width)),
                whole((1, width)),
                pl.BlockSpec((1, 8, two // 2), lambda c, *_: (c, 0, 0)),
                whole((1, width)),
                whole((1, width)),
            ],
            scratch_shapes=[pltpu.VMEM((rows, width), F32)],
        ),
        compiler_params=pltpu.CompilerParams(vmem_limit_bytes=48 << 20),
        cost_estimate=pl.CostEstimate(
            flops=15 * rows * w.size + 12 * rows * proj.size, bytes_accessed=4 * w.size, transcendentals=0
        ),
        name="mlp_back",
    )(group_ids, grad, after, normed, gain, proj, w, bup, *atts)


def padded(blk):
    return -(-blk // 128) * 128


def heads_apart(cat_ref, block):
    blk, width = block.shape
    wide = block.astype(F32)
    lane = lax.broadcasted_iota(jnp.int32, (blk, width), 1)
    for h in range(width // HEAD_DIM):
        mine = (lane >= h * HEAD_DIM) & (lane < (h + 1) * HEAD_DIM)
        at = h * padded(blk)
        cat_ref[at : at + blk, :] = jnp.where(mine, wide, 0.0).astype(BF)


def causal_tile(blk, heads):
    pad = padded(blk)
    key_at = lax.broadcasted_iota(jnp.int32, (blk, heads * pad), 0)
    query_at = lax.broadcasted_iota(jnp.int32, (blk, heads * pad), 1)
    return key_at <= lax.rem(query_at, pad)


def query_part(ref, rows, width):
    low = width // 128 * 128
    high = -(-2 * width // 128) * 128
    window = ref[rows, low:high].astype(F32)
    if width > low:
        window = pltpu.roll(window, high - width, 1)
    return (window[:, :width] * (HEAD_DIM ** (-0.5))).astype(BF)


def attend_kernel(q_id, k_loc, *refs):
    mixed_refs, o_refs, (lse_ref, *scratch) = split_refs(
        refs, len(refs) - GROUPS - 8, GROUPS, 8
    )
    q_ref, k_ref, vt_ref, acc_ref, cat_ref, even_ref, odd_ref = scratch
    q_blocks, blk, width = q_ref.shape
    heads = width // HEAD_DIM

    for r, ref in enumerate(mixed_refs):
        for b in range(2):
            rows = slice(b * blk, (b + 1) * blk)
            k_ref[2 * r + b] = ref[rows, :width]
            vt_ref[2 * r + b] = ref[rows, 2 * width :].astype(F32).T.astype(BF)
            if r < GROUPS:
                q_ref[2 * r + b] = query_part(ref, rows, width)
    pad = padded(blk)
    cat_ref[...] = jnp.zeros_like(cat_ref)
    head_rows = [slice(h * HEAD_DIM, (h + 1) * HEAD_DIM) for h in range(heads)]
    head_cols = [slice(h * pad, (h + 1) * pad) for h in range(heads)]

    def per_query(qb):
        heads_apart(cat_ref, q_ref[qb])
        own = q_id[qb]
        loc = k_loc[own]
        even_ref[...] = jnp.where(
            causal_tile(blk, heads), dot_nt(k_ref[loc], cat_ref[...]), -1e30
        )
        acc_ref[...] = jnp.zeros_like(acc_ref)

        def block_at(t):
            return k_loc[jnp.where(t == 0, own, jnp.minimum(t, own) - 1 + (own == 0))]

        def half(t, here, ahead, carry):
            top, total = carry
            ahead[...] = dot_nt(k_ref[block_at(t + 1)], cat_ref[...])
            s = here[...] + jnp.where(t <= own, 0.0, -1e30)
            new = jnp.maximum(top, jnp.max(s, axis=0, keepdims=True))
            alpha = jnp.exp(top - new)
            p = jnp.exp(s - new)
            total = total * alpha + jnp.sum(p, axis=0, keepdims=True)
            p = p.astype(BF)
            loc = block_at(t)
            for h in range(heads):
                acc_ref[head_rows[h], :] = acc_ref[head_rows[h], :] * alpha[
                    :, head_cols[h]
                ] + dot_nn(vt_ref[loc, head_rows[h], :], p[:, head_cols[h]])
            return new, total

        def step(i, carry):
            carry = half(2 * i, even_ref, odd_ref, carry)
            return half(2 * i + 1, odd_ref, even_ref, carry)

        row = (1, heads * pad)
        start = (jnp.full(row, -1e30, F32), jnp.zeros(row, F32))
        top, total = lax.fori_loop(0, own // 2 + 1, step, start)
        for h in range(heads):
            acc_ref[head_rows[h], :] = acc_ref[head_rows[h], :] / total[:, head_cols[h]]
        lse_ref[qb, :1, :] = top + jnp.log(total)
        return acc_ref[...].T[:blk].astype(BF)

    for k in range(GROUPS):

        def pair(b, _, k=k):
            start = pl.multiple_of(b * blk, 32)
            o_refs[k][pl.ds(start, blk), :] = per_query(2 * k + b)
            return 0

        lax.fori_loop(0, 2, pair, 0)


def attend(q_id, k_loc, mixed):
    rows, cols = mixed[0].shape
    blk, width = rows // 2, cols // 3
    q_blocks, k_blocks = 2 * GROUPS, 2 * len(mixed)
    return pl.pallas_call(
        attend_kernel,
        out_shape=[jax.ShapeDtypeStruct((rows, width), BF)] * GROUPS
        + [jax.ShapeDtypeStruct((q_blocks, 8, width // HEAD_DIM * padded(blk)), F32)],
        grid_spec=pltpu.PrefetchScalarGridSpec(
            num_scalar_prefetch=2,
            grid=(1,),
            in_specs=[whole(x.shape) for x in mixed],
            out_specs=[whole((rows, width))] * GROUPS
            + [whole((q_blocks, 8, width // HEAD_DIM * padded(blk)))],
            scratch_shapes=[
                pltpu.VMEM((q_blocks, blk, width), BF),
                pltpu.VMEM((k_blocks, blk, width), BF),
                pltpu.VMEM((k_blocks, width, blk), BF),
                pltpu.VMEM((width, padded(blk)), F32),
                pltpu.VMEM((width // HEAD_DIM * padded(blk), width), BF),
                pltpu.VMEM((blk, width // HEAD_DIM * padded(blk)), F32),
                pltpu.VMEM((blk, width // HEAD_DIM * padded(blk)), F32),
            ],
        ),
        compiler_params=pltpu.CompilerParams(vmem_limit_bytes=48 << 20),
        cost_estimate=pl.CostEstimate(
            flops=28 * q_blocks * k_blocks * blk * blk * width,
            bytes_accessed=2 * len(mixed) * rows * cols,
            transcendentals=q_blocks * k_blocks * blk * blk * 2,
        ),
        name="attend",
    )(q_id, k_loc, *mixed)


def attend_back_kernel(q_id, key_ids, *refs):
    count = (len(refs) - 2 * GROUPS - 11) // 2
    mixed_refs, o_refs, do_refs, (lse_ref,), dm_refs, scratch = split_refs(
        refs, count, GROUPS, GROUPS, 1, count, 10
    )
    q_ref, k_ref, v_ref, kt_ref, dq_ref, dka_ref, dva_ref, dqt_ref, cat_ref, dcat_ref = scratch
    q_blocks, blk, width = q_ref.shape
    heads = width // HEAD_DIM
    for r, ref in enumerate(mixed_refs):
        for b in range(2):
            rows = slice(b * blk, (b + 1) * blk)
            at = key_ids[2 * r + b]
            in_order = pl.ds(pl.multiple_of(at * blk, 32), blk)
            keys = ref[rows, :width]
            k_ref[in_order, :] = keys
            kt_ref[at] = keys.astype(F32).T.astype(BF)
            v_ref[in_order, :] = ref[rows, 2 * width :]
            if r < GROUPS:
                q_ref[2 * r + b] = query_part(ref, rows, width)

    def clear(b, _):
        rows = pl.ds(pl.multiple_of(b * blk, 32), blk)
        dka_ref[rows, :] = jnp.zeros((blk, width), F32)
        dva_ref[rows, :] = jnp.zeros((blk, width), F32)
        return 0

    lax.fori_loop(0, kt_ref.shape[0], clear, 0)
    pad = padded(blk)
    cat_ref[...] = jnp.zeros_like(cat_ref)
    dcat_ref[...] = jnp.zeros_like(dcat_ref)

    def per_query(qb, do_blk, o_blk):
        heads_apart(cat_ref, q_ref[qb])
        heads_apart(dcat_ref, do_blk)
        both = do_blk.astype(F32) * o_blk.astype(F32)
        both = jnp.concatenate([both, jnp.zeros((pad - blk, width), F32)], 0).T
        delta = jnp.concatenate(
            [
                jnp.sum(both[h * HEAD_DIM : (h + 1) * HEAD_DIM], axis=0, keepdims=True)
                for h in range(heads)
            ],
            1,
        )
        lse = lse_ref[qb, :1, :]
        own = q_id[qb]

        dqt_ref[...] = jnp.zeros_like(dqt_ref)

        def two_blocks(t, allowed):
            rows = pl.ds(pl.multiple_of(t * (2 * blk), 32), 2 * blk)
            p = jnp.exp(dot_nt(k_ref[rows, :], cat_ref[...]) - lse)
            if allowed is not None:
                p = jnp.where(allowed, p, 0.0)
            dp = dot_nt(v_ref[rows, :], dcat_ref[...])
            ds = (p * (dp - delta)).astype(BF)
            dva_ref[rows, :] += dot_nn(p.astype(BF), dcat_ref[...])
            dka_ref[rows, :] += dot_nn(ds, cat_ref[...])
            for h in range(heads):
                part = slice(h * HEAD_DIM, (h + 1) * HEAD_DIM)
                cols = slice(h * pad, (h + 1) * pad)
                dqt_ref[part, :] += dot_nn(kt_ref[2 * t, part, :], ds[:blk, cols]) + dot_nn(
                    kt_ref[2 * t + 1, part, :], ds[blk:, cols]
                )

        def step(t, _):
            two_blocks(t, None)
            return 0

        last = own // 2
        lax.fori_loop(0, last, step, 0)
        shape = (2 * blk, heads * pad)
        key_at = lax.broadcasted_iota(jnp.int32, shape, 0)
        query_at = lax.rem(lax.broadcasted_iota(jnp.int32, shape, 1), pad)
        two_blocks(last, key_at - query_at <= (own - 2 * last) * blk)
        dq_ref[qb] = (dqt_ref[...] * (HEAD_DIM ** (-0.5))).T[:blk]

    for k in range(GROUPS):

        def pair(b, _, k=k):
            rows = pl.ds(pl.multiple_of(b * blk, 32), blk)
            per_query(2 * k + b, do_refs[k][rows, :], o_refs[k][rows, :])
            return 0

        lax.fori_loop(0, 2, pair, 0)

    for r, ref in enumerate(dm_refs):

        def finish(b, _, r=r, ref=ref):
            rows = pl.ds(pl.multiple_of(key_ids[2 * r + b] * blk, 32), blk)
            dq = dq_ref[2 * r + b] if r < GROUPS else jnp.zeros((blk, width), F32)
            joined = jnp.concatenate([dka_ref[rows, :], dq, dva_ref[rows, :]], 1)
            ref[pl.ds(pl.multiple_of(b * blk, 32), blk), :] = joined.astype(BF)
            return 0

        lax.fori_loop(0, 2, finish, 0)


def attend_back(q_id, key_ids, mixed, o, do, lse):
    rows, cols = mixed[0].shape
    blk, width = rows // 2, cols // 3
    q_blocks, k_blocks = 2 * GROUPS, 2 * len(mixed)
    return pl.pallas_call(
        attend_back_kernel,
        out_shape=[jax.ShapeDtypeStruct((rows, cols), BF)] * len(mixed),
        grid_spec=pltpu.PrefetchScalarGridSpec(
            num_scalar_prefetch=2,
            grid=(1,),
            in_specs=[whole(x.shape) for x in (*mixed, *o, *do, lse)],
            out_specs=[whole((rows, cols))] * len(mixed),
            scratch_shapes=[
                pltpu.VMEM((q_blocks, blk, width), BF),
                pltpu.VMEM((k_blocks * blk, width), BF),
                pltpu.VMEM((k_blocks * blk, width), BF),
                pltpu.VMEM((k_blocks, width, blk), BF),
                pltpu.VMEM((q_blocks, blk, width), F32),
                pltpu.VMEM((k_blocks * blk, width), F32),
                pltpu.VMEM((k_blocks * blk, width), F32),
                pltpu.VMEM((width, padded(blk)), F32),
                pltpu.VMEM((width // HEAD_DIM * padded(blk), width), BF),
                pltpu.VMEM((width // HEAD_DIM * padded(blk), width), BF),
            ],
        ),
        compiler_params=pltpu.CompilerParams(vmem_limit_bytes=56 << 20),
        cost_estimate=pl.CostEstimate(
            flops=48 * q_blocks * k_blocks * blk * blk * width,
            bytes_accessed=4 * len(mixed) * rows * cols,
            transcendentals=q_blocks * k_blocks * blk * blk * 2,
        ),
        name="attend_back",
    )(q_id, key_ids, *mixed, *o, *do, lse)


def swap(x, axis_name, size, k):
    return lax.ppermute(x, axis_name, [(i, i ^ k) for i in range(size)])


def pick(x, at):
    return lax.dynamic_index_in_dim(x, at, 0, keepdims=False)


class Place:
    def __init__(self, n, m):
        self.n, self.m = n, m
        self.inner = n // GROUPS
        self.idx = lax.axis_index("ctx")
        self.outer_at = self.idx // self.inner
        self.inner_at = self.idx % self.inner
        self.w = lax.axis_index("wt")

    def exchange(self, parts):
        return [parts[0]] + [
            swap(parts[k], "ctx", self.n, k * self.inner) for k in range(1, GROUPS)
        ]

    def scatter_ctx(self, x):
        return lax.psum_scatter(x, "ctx", scatter_dimension=0, tiled=True)

    def gather_ctx(self, x):
        return lax.all_gather(x, "ctx", axis=0, tiled=False)

    def scatter_wt(self, x):
        total = pick(x, self.w).astype(F32)
        for k in range(1, self.m):
            total = total + swap(pick(x, self.w ^ k), "wt", self.m, k).astype(F32)
        return total

    def total(self, x):
        for axis_name, size in (("ctx", self.n), ("wt", self.m)):
            k = 1
            while k < size:
                x = x + swap(x, axis_name, size, k)
                k *= 2
        return x


def split_columns(shard, at, count, groups):
    rows, cols = shard.shape
    c = cols // (groups * count)
    cut = shard.reshape(rows, groups, count, c)
    return lax.dynamic_index_in_dim(cut, at, 2, keepdims=False).reshape(rows, groups * c)


def qkv_piece(shard, place):
    rows, cols = shard.shape
    cut = shard.reshape(rows, 3, GROUPS, cols // (3 * GROUPS))
    own = lax.dynamic_index_in_dim(cut, place.outer_at, 2, keepdims=False)
    own = jnp.concatenate([own[:, 1], own[:, 0], own[:, 2]], 1)
    part = own.shape[1] // place.inner
    return lax.dynamic_slice_in_dim(own, place.inner_at * part, part, 1)


def after(x, done):
    return lax.optimization_barrier((x, done))[0]


def pack_layer(place, matrices, layer):
    qkv_weight, out_weight, up_weight, down_weight = matrices
    n, m = place.n, place.m
    width, ff = out_weight.shape[2], up_weight.shape[2]
    columns = jnp.concatenate(
        [
            qkv_piece(qkv_weight[layer], place),
            split_columns(out_weight[layer], place.idx, n, 1),
            split_columns(up_weight[layer], place.idx, n, m),
        ],
        1,
    )
    pad = -columns.shape[1] % width
    assert pad == 0 or columns.shape[1] < width
    if pad:
        columns = jnp.pad(columns, ((0, 0), (0, pad)))
    down = pick(down_weight[layer].reshape(n, ff // (n * m), width), place.idx)
    return jnp.concatenate([columns, down], 0)


def pack_small(small, width):
    flat = [s.reshape(-1) for s in small]
    size = sum(f.shape[0] for f in flat)
    extra = -(-size // (width * 16)) * 16
    flat.append(jnp.zeros((extra * width - size,), BF))
    return jnp.concatenate(flat).reshape(extra, width)


def unpack_small(place, parts, small):
    got = jnp.stack([pick(jnp.stack(parts), place.w ^ i) for i in range(place.m)])
    got = got.reshape(place.m, -1)
    out, at = [], 0
    for s in small:
        count, c = s.shape
        part = got[:, at : at + count * c].reshape(place.m, count, c)
        out.append(part.transpose(1, 0, 2).reshape(count, place.m * c).astype(F32))
        at += count * c
    return out


def spread_wt(place, x):
    return [x] + [swap(x, "wt", place.m, k) for k in range(1, place.m)]


def scatter_part(place, dw):
    return place.scatter_ctx(dw.reshape(-1, dw.shape[2]))


def own_part(place, part, kernel, rows):
    turned = turn(kernel, part, (place.m, rows, part.size // (place.m * rows)))
    return place.scatter_wt(turned).astype(BF)


def unpack_feed(place, own, ff, width):
    n, m = place.n, place.m
    rows = width // m
    up, down = own[:, :rows], own[:, rows:]
    up = up.reshape(n, rows, m, ff // (n * m)).transpose(1, 2, 0, 3).reshape(rows, ff)
    down = down.reshape(n, -1, ff // (n * m), down.shape[2]).transpose(0, 2, 1, 3)
    return up.astype(F32), down.reshape(ff // m, width).astype(F32)


def unpack_attn(place, own, width):
    n, m = place.n, place.m
    rows = 3 * width // n
    gw = width // GROUPS
    qkv, proj = own[:, :, :rows], own[:, :, rows:]
    qkv = qkv.reshape(GROUPS, place.inner, width // m, rows).transpose(2, 0, 1, 3)
    qkv = qkv.reshape(width // m, GROUPS, 3, gw)
    qkv = jnp.concatenate([qkv[:, :, i].reshape(width // m, width) for i in (1, 0, 2)], 1)
    proj = proj.transpose(1, 0, 2).reshape(width // m, width)
    return qkv.astype(F32), proj.astype(F32)


def reduce_small(place, smalls):
    sizes = [v.shape[0] for v in smalls[0]]
    packed = jnp.concatenate([v for layer in smalls for v in layer]).reshape(-1, 128)
    packed = place.total(packed).reshape(len(smalls), -1)
    out, at = [], 0
    for size in sizes:
        part = packed[:, at : at + size].reshape(len(smalls), place.m, size // place.m)
        out.append(lax.dynamic_index_in_dim(part, place.w, 1, keepdims=False))
        at += size
    return out


def body(
    n, m, inputs, block_table, ln1_gain, ln1_bias, qkv_weight, query_bias, value_bias, out_weight,
    out_bias, ln2_gain, ln2_bias, up_weight, up_bias, down_weight, down_bias, cotangent,
):
    place = Place(n, m)
    rows, width = inputs.shape[1:]
    ff = up_weight.shape[2]
    gw = width // GROUPS
    group_ids = jnp.stack([place.outer_at ^ k for k in range(GROUPS)]).astype(jnp.int32)
    key_ids = jnp.concatenate(
        [
            pick(block_table, place.idx ^ (k * place.inner + j))
            for j in range(place.inner)
            for k in range(GROUPS)
        ]
    ).astype(jnp.int32)
    q_id = key_ids[: 2 * GROUPS]
    at = jnp.arange(2 * n, dtype=jnp.int32)
    k_loc = jnp.sum(jnp.where(key_ids[None, :] == at[:, None], at[None, :], 0), axis=1).astype(jnp.int32)

    small = (ln1_gain, ln1_bias, query_bias, value_bias, out_bias, ln2_gain, ln2_bias, up_bias, down_bias)
    matrices = (qkv_weight, out_weight, up_weight, down_weight)
    w_at = place.w.astype(jnp.int32).reshape(1)
    attn_rows, feed_rows = 4 * width // n, 2 * ff // n
    big_rows = width // m + ff // (n * m)
    first = jnp.concatenate([pack_layer(place, matrices, 0), pack_small(small, width)], 0)
    parts = spread_wt(place, first)
    vectors = unpack_small(place, [p[big_rows:] for p in parts], small)
    attn, feed = turn_weights(w_at, parts, attn_rows, feed_rows)
    attn = place.gather_ctx(attn)
    weights = [(attn, place.gather_ctx(after(feed, attn)))]
    params = []
    for layer in range(LAYERS):
        v = [x[layer].reshape(1, -1) for x in vectors]
        bias = jnp.concatenate(
            [jnp.zeros((GROUPS, 1, gw), F32), v[2].reshape(GROUPS, 1, gw), v[3].reshape(GROUPS, 1, gw)], 2
        )
        bup = v[7].reshape(m, n, ff // (n * m)).transpose(1, 0, 2).reshape(n, 1, ff // n)
        params.append((v, bias, bup))

    state = inputs[0].astype(F32)
    saved = []
    for layer in range(LAYERS):
        attn, feed = weights[layer]
        v, bias, bup = params[layer]
        *mixed, normed, proj = mix(group_ids, state, v[0], v[1], attn, bias)
        mixed = place.exchange(mixed)
        if layer + 1 < LAYERS:
            send = after(pack_layer(place, matrices, layer + 1), parts[1])
            parts = spread_wt(place, send)
        mixed = mixed + [
            swap(x, "ctx", n, j) for j in range(1, place.inner) for x in mixed
        ]
        *o, lse = attend(q_id, k_loc, mixed)
        if layer + 1 < LAYERS:
            next_attn, next_feed = turn_weights(w_at, parts, attn_rows, feed_rows)
            next_attn = place.gather_ctx(after(next_attn, (feed, mixed)))
            weights.append((next_attn, place.gather_ctx(after(next_feed, (next_attn, o[0])))))
        atts = place.exchange(o)
        mid, normed_two, new = mlp(
            group_ids, state, proj, v[4], v[5], v[6], feed, bup, v[8], atts
        )
        saved.append((state, normed, mixed, o, lse, atts, mid, normed_two, proj))
        state = new
    outputs = state.astype(BF)[None]
    gradient = cotangent[0].astype(F32)
    shards, smalls, pending = [None] * LAYERS, [None] * LAYERS, []
    for layer in reversed(range(LAYERS)):
        attn, feed = weights[layer]
        v, bias, bup = params[layer]
        before, normed, mixed, o, lse, atts, mid, normed_two, proj = saved[layer]
        *datts, dfeed, dproj, gafter, dgain2, dshift2, dbup, dbdown, dbproj = mlp_back(
            group_ids, gradient, mid, normed_two, v[5], proj, feed, bup, atts
        )
        part_feed = scatter_part(place, dfeed)
        do = place.exchange(datts)
        dm = attend_back(q_id, key_ids, mixed, o, do, lse)
        dm = list(dm)
        if layer > 0:
            dm[0] = after(dm[0], part_feed)
        if layer + 1 < LAYERS:
            part_attn = after(part_attn, dm[1])
            pending.append(own_part(place, part_attn, turn_attn_kernel, width // m))
        part_feed = after(part_feed, dm[1])
        pending.append(own_part(place, part_feed, turn_feed_kernel, 2 * width // m))
        own = []
        for k in range(GROUPS):
            if place.inner == 1:
                own.append(dm[k])
                continue
            total = dm[k].astype(F32)
            for j in range(1, place.inner):
                total = total + swap(dm[j * GROUPS + k], "ctx", n, j).astype(F32)
            own.append(total.astype(BF))
        gms = place.exchange(own)
        dmix, gradient, dgain1, dshift1, dbias = mix_back(
            group_ids, gafter, before, v[0], normed, attn, dproj, gms
        )
        if layer == 0:
            joined = place.gather_ctx(jnp.concatenate(pending, 0))
            dmix = after(dmix, joined)
        part_attn = scatter_part(place, dmix)
        dbup = dbup[:, 0].reshape(n, m, ff // (n * m)).transpose(1, 0, 2)
        smalls[layer] = [
            x.reshape(-1)
            for x in (
                dgain1, dshift1, dbias[:, 0, gw : 2 * gw], dbias[:, 0, 2 * gw :], dbproj,
                dgain2, dshift2, dbup, dbdown,
            )
        ]
    own_attn = place.gather_ctx(own_part(place, part_attn, turn_attn_kernel, width // m))
    counts, at, owns = [p.shape[0] for p in pending], 0, []
    for count in counts:
        owns.append(joined[:, at : at + count])
        at += count
    for layer in range(LAYERS):
        own_feed = owns[2 * (LAYERS - 1 - layer)]
        part = own_attn if layer == 0 else owns[2 * (LAYERS - 1 - layer) + 1]
        shards[layer] = unpack_attn(place, part, width) + unpack_feed(place, own_feed, ff, width)
    vec = reduce_small(place, smalls)
    mixw, projw, up, down = [jnp.stack([s[i] for s in shards]) for i in range(4)]
    return (
        outputs, gradient[None], vec[0], vec[1], mixw, vec[2], vec[3], projw, vec[4],
        vec[5], vec[6], up, vec[7], down, vec[8],
    )


def solution(mesh):
    row, vec, mat = P("wt", "ctx", None), P(None, "wt"), P(None, "wt", None)
    in_specs = (row, P(), vec, vec, mat, vec, vec, mat, vec, vec, vec, mat, vec, mat, vec, row)
    out_specs = (row, row, vec, vec, mat, vec, vec, mat, vec, vec, vec, mat, vec, mat, vec)
    return jax.shard_map(
        functools.partial(body, mesh.shape["ctx"], mesh.shape["wt"]),
        mesh=mesh,
        in_specs=in_specs,
        out_specs=out_specs,
        check_vma=False,
    )
```
